32 devices in a mesh: space: 16 (over z, y, x), wt: 2 (over core).
Axes of the slice: x: 2, y: 2, z: 4, core: 2. Of those that a mesh axis runs over, the one named last changes fastest.
Arguments:
- features: bfloat16 [32, 8, 8, 8, 192], P(('space', 'wt')), may hold values from -6 to 6
- occupancy: int32 [32], P(('space', 'wt')), may hold values from 0 to 1, as said below
- neighbours: int32 [32, 27], P(('space', 'wt')), may hold values from -1 to 31, as said below
- kernel_one: bfloat16 [3, 3, 3, 48, 768], P(None, None, None, None, 'wt'), may hold values from -0.078125 to 0.078125
- kernel_two: bfloat16 [3, 3, 3, 48, 768], P(None, None, None, None, 'wt'), may hold values from -0.078125 to 0.078125
Outputs:
- block_out: float32 [32, 8, 8, 8, 192], P(('space', 'wt'))
The draws below stay inside these ranges and needn't reach their ends.
Inputs may be any that keep to these rules, and one draw needn't show every extreme that they name: `occupancy`: the first slot of every device's 1 slots is active; the others are active with probability three quarters. `neighbours`: entries are -1 or an active slot; for an active slot s, entry 13 is s itself, and every other entry lies among the slots of the same device, the previous or the next device in slot order (slots d * 1 to (d+1) - 1 belong to device d). Rows of inactive slots are all -1.
All inputs are finite; a program needn't handle non-finite values.
Results may differ from the reference program's by a relative error of at most 0.0018.
Values may be sent and summed in bfloat16 or wider, within the bound.
No kernel may reach another device: no remote copies, remote signals or barrier semaphores. Data moves between devices by JAX's collectives and lax.ppermute only.
A program may use at most 64 MiB of HBM per device.

```python
import jax
import jax.numpy as jnp
from jax import lax

C = 192
BLK_DEV = 1
SLOTS = 32


def common_blocks(key):
    key_occ = jax.random.fold_in(key, 101)
    key_pick = jax.random.fold_in(key, 202)
    key_slot = jax.random.fold_in(key, 303)
    key_miss = jax.random.fold_in(key, 404)
    slot_ids = jnp.arange(SLOTS, dtype=jnp.int32)
    occupied = (jax.random.randint(key_occ, (SLOTS,), 0, 4) > 0) | (slot_ids % BLK_DEV == 0)
    device_ids = slot_ids // BLK_DEV
    step_dev = jax.random.randint(key_pick, (SLOTS, 27), -1, 2)
    inner = jax.random.randint(key_slot, (SLOTS, 27), 0, BLK_DEV)
    candidate = (device_ids[:, None] + step_dev) * BLK_DEV + inner
    inside = (candidate >= 0) & (candidate < SLOTS)
    safe = jnp.clip(candidate, 0, SLOTS - 1)
    keep = jax.random.randint(key_miss, (SLOTS, 27), 0, 5) > 0
    valid = inside & occupied[safe] & keep
    table = jnp.where(valid, safe, -1)
    table = table.at[:, 13].set(slot_ids)
    table = jnp.where(occupied[:, None], table, -1)
    return (occupied.astype(jnp.int32), table.astype(jnp.int32))


def draw_occupancy(key, part):
    return common_blocks(key)[0]


def draw_neighbours(key, part):
    return common_blocks(key)[1]


def block_scale(stream_key, extent, split, low, top_value):
    def one(dim, shards_of):
        draws = jax.random.uniform(jax.random.fold_in(jax.random.fold_in(stream_key, 6), dim), (shards_of,), jnp.float32, low / len(split), top_value / len(split))
        return jnp.repeat(jnp.exp(draws), extent[dim] // shards_of).reshape((-1,) + (1,) * (len(extent) - dim - 1))

    loudness = one(*split[0])
    for cut in split[1:]:
        loudness = loudness * one(*cut)
    return loudness


def normal_values(own_key, shape, scale, limit, shards=(), kind=jnp.bfloat16):
    values = scale * jax.random.normal(own_key, shape, jnp.float32)
    if shards:
        values = values * block_scale(own_key, shape, shards, -0.22, 0.18)
    return jnp.clip(values, -limit, limit).astype(kind)


def setup_inputs(seed: int = 0) -> dict:
    seeds = jax.random.split(jax.random.key(seed), 6)
    return {
        "features": normal_values(seeds[0], (SLOTS, 8, 8, 8, C), 1.0, 6.0, ((0, 32),)),
        "occupancy": draw_occupancy(jax.random.fold_in(seeds[5], 71), 0),
        "neighbours": draw_neighbours(jax.random.fold_in(seeds[5], 71), 0),
        "kernel_one": normal_values(seeds[3], (3, 3, 3, C // 4, 4 * C), (27 * C) ** -0.5, 0.078125, ((4, 2),)),
        "kernel_two": normal_values(seeds[4], (3, 3, 3, C // 4, 4 * C), (27 * C) ** -0.5, 0.078125, ((4, 2),)),
    }


def unpack_kernel(stored):
    quarter = stored.shape[3]
    width = stored.shape[4] // 4
    grouped = stored.reshape(3, 3, 3, quarter, 4, width)
    return jnp.transpose(grouped, (0, 1, 2, 4, 3, 5)).reshape(3, 3, 3, 4 * quarter, width)


def pad_blocks(source, index):
    ranges = ((7, 8), (0, 8), (0, 1))
    planes = []
    for first in range(3):
        rows = []
        for second in range(3):
            cols = []
            for third in range(3):
                tap = first * 9 + second * 3 + third
                which = index[:, tap]
                picked = jnp.take(source, jnp.maximum(which, 0).astype(jnp.int32), axis=0)
                lo_a, hi_a = ranges[first]
                lo_b, hi_b = ranges[second]
                lo_c, hi_c = ranges[third]
                piece = picked[:, lo_a:hi_a, lo_b:hi_b, lo_c:hi_c, :]
                valid = (which >= 0)[:, None, None, None, None]
                cols.append(jnp.where(valid, piece, jnp.zeros((), piece.dtype)))
            rows.append(jnp.concatenate(cols, axis=3))
        planes.append(jnp.concatenate(rows, axis=2))
    return jnp.concatenate(planes, axis=1)


def conv_taps(padded, kernel):
    return lax.conv_general_dilated(padded.astype(jnp.float32), kernel.astype(jnp.float32), (1, 1, 1), "VALID", dimension_numbers=("NDHWC", "DHWIO", "NDHWC"), precision=lax.Precision.HIGHEST)


def apply_layer(source, neighbours, kernel):
    groups = SLOTS // BLK_DEV

    def one_group(group):
        index = lax.dynamic_slice_in_dim(neighbours, (group * BLK_DEV).astype(jnp.int32), BLK_DEV, 0)
        return conv_taps(pad_blocks(source, index), kernel)

    result = lax.map(one_group, jnp.arange(groups, dtype=jnp.int32))
    return result.reshape(source.shape[0], 8, 8, 8, kernel.shape[4])


def reference(features, occupancy, neighbours, kernel_one, kernel_two):
    active = occupancy.astype(jnp.float32)[:, None, None, None, None]
    hidden = (jax.nn.relu(apply_layer(features, neighbours, unpack_kernel(kernel_one))) * active).astype(jnp.bfloat16)
    return jax.nn.relu(features.astype(jnp.float32) + apply_layer(hidden, neighbours, unpack_kernel(kernel_two))) * active
```

```python
import functools

import jax
import jax.numpy as jnp
from jax import lax
from jax.experimental import pallas as pl
from jax.experimental.pallas import tpu as pltpu
from jax.sharding import PartitionSpec as P

AXES = ("space", "wt")
VMEM = pltpu.VMEM
SMEM = pltpu.SMEM


def surface_rows(side):
    plane = side * side
    inner = (side - 2) * side
    return 2 * plane + 4 * inner


LANES = 128


def pieces(width):
    return [(p, p * LANES, min(LANES, width - p * LANES)) for p in range(-(-width // LANES))]


def fill(wide, base, value):
    rows, width = value.shape
    for p, lane, lanes in pieces(width):
        wide[p, pl.ds(base, rows), 0:lanes] = value[:, lane : lane + lanes]


def pack_surface(wide, base, out_ref, side):
    plane = side * side
    inner = (side - 2) * side
    last = side - 1

    for p, lane, lanes in pieces(out_ref.shape[1]):
        ref = wide.at[p]

        def store(row, value):
            out_ref[pl.ds(row, value.shape[0]), lane : lane + lanes] = value[
                :, :lanes
            ].astype(jnp.bfloat16)

        store(0, ref[pl.ds(base, plane), :])
        store(plane, ref[pl.ds(base + last * plane, plane), :])
        row = 2 * plane
        for y in (0, last):
            parts = [
                ref[pl.ds(base + x * plane + y * side, side), :]
                for x in range(1, last)
            ]
            store(row, jnp.concatenate(parts, axis=0))
            row += inner
        for z in (0, last):
            store(row, ref[pl.ds(base + plane + z, inner, stride=side), :])
            row += inner


def unpack_surface(far_ref, wide, base, side):
    plane = side * side
    inner = (side - 2) * side
    last = side - 1
    far = far_ref[...].astype(jnp.float32)
    for p, lane, lanes in pieces(far.shape[1]):
        ref = wide.at[p]
        part = far[:, lane : lane + lanes]
        if lanes < LANES:
            pad = jnp.zeros((far.shape[0], LANES - lanes), jnp.float32)
            part = jnp.concatenate([part, pad], axis=1)
        ref[pl.ds(base, plane), :] = part[0:plane]
        ref[pl.ds(base + last * plane, plane), :] = part[plane : 2 * plane]
        row = 2 * plane
        for y in (0, last):
            for x in range(1, last):
                at = row + (x - 1) * side
                ref[pl.ds(base + x * plane + y * side, side), :] = part[at : at + side]
            row += inner
        for z in (0, last):
            ref[pl.ds(base + plane + z, inner, stride=side), :] = part[
                row : row + inner
            ]
            row += inner


def pack_kernel(x_ref, out_ref, wide, *, side):
    fill(wide, 0, x_ref[...].astype(jnp.float32))
    pack_surface(wide, 0, out_ref, side)


def weights_kernel(own_ref, other_ref, out_ref):
    core = lax.axis_index("wt")
    taps, depth, both = own_ref.shape
    width = out_ref.shape[2]
    half = depth * (both // width)
    for ref, place in ((own_ref, core), (other_ref, 1 - core)):
        for group in range(both // width):
            row = pl.multiple_of(place * half + group * depth, 16)
            out_ref[:, pl.ds(row, depth), :] = ref[
                :, :, group * width : (group + 1) * width
            ]


def conv(table, block, center, beside, far_ref, w_ref, src, even, odd, side):
    rows, width = center.shape
    plane = side * side
    last = side - 1
    fill(src, 0, jnp.zeros((rows, width), jnp.float32))
    fill(src, rows, beside[...].astype(jnp.float32))
    fill(src, 2 * rows, center[...].astype(jnp.float32))
    unpack_surface(far_ref, src, 3 * rows, side)

    def slot(a, b, c):
        if (a, b, c) == (0, 0, 0):
            return 2
        n = table[0, 9 * (a + 1) + 3 * (b + 1) + c + 1]
        near = jnp.where(n == block, 2, jnp.where(n == block + 1 - 2 * (block % 2), 1, 3))
        return jnp.where(n < 0, 0, near)

    slots = {
        (a, b, c): slot(a, b, c)
        for a in (-1, 0, 1)
        for b in (-1, 0, 1)
        for c in (-1, 0, 1)
    }

    def span(index):
        if index == 0:
            return -1, last
        if index == side + 1:
            return 1, 0
        return 0, index - 1

    z = lax.broadcasted_iota(jnp.int32, (side, side, LANES), 1)
    for xx in range(side + 2):
        a, x = span(xx)
        for b, y, count, to in ((-1, last, 1, 0), (0, 0, side, 1), (1, 0, 1, side + 1)):
            for p, lane, lanes in pieces(width):

                def chunk(c):
                    start = slots[a, b, c] * rows + x * plane + y * side
                    if not isinstance(start, int):
                        start = pl.multiple_of(start, side)
                    return src[p, pl.ds(start, count * side), :].reshape(
                        count, side, LANES
                    )

                middle = chunk(0)
                mask = z[:count]
                low = jnp.where(mask == last, chunk(-1), middle)
                high = jnp.where(mask == 0, chunk(1), middle)
                shifted = (
                    pltpu.roll(low, 1, axis=1),
                    middle,
                    pltpu.roll(high, side - 1, axis=1),
                )
                for k in range(3):
                    value = shifted[k].reshape(count * side, LANES)[:, :lanes]
                    even[
                        k, xx, pl.ds(to * side, count * side), lane : lane + lanes
                    ] = value
                    if b == 0:
                        odd[k, xx, :, lane : lane + lanes] = value.astype(jnp.bfloat16)


def conv_sum(even, evenb, odd, w_ref, rows, width, side):
    plane = side * side
    evenb[...] = even[...].astype(jnp.bfloat16)
    acc = jnp.zeros((rows, width), jnp.float32)
    for i in range(3):
        for j in range(3):
            for k in range(3):
                if j == 1:
                    part = odd[k, i : i + side]
                else:
                    part = evenb[k, i : i + side, j * side : j * side + plane]
                acc += jnp.dot(
                    part.reshape(rows, width),
                    w_ref[9 * i + 3 * j + k],
                    preferred_element_type=jnp.float32,
                )
    return acc


def first_kernel(
    table, occupancy, center, beside, far, w, out, surface, src, even, evenb, odd, *, side
):
    core = lax.axis_index("wt")
    block = 2 * lax.axis_index("space") + 1 - core
    rows, width = center.shape
    conv(table, block, center, beside, far, w, src, even, odd, side)
    acc = conv_sum(even, evenb, odd, w, rows, width, side)
    hidden = jnp.maximum(acc, 0.0) * occupancy[0, 0].astype(jnp.float32)
    out[...] = hidden.astype(jnp.bfloat16)
    fill(src, 0, hidden)
    pack_surface(src, 0, surface, side)


def second_kernel(
    table, occupancy, center, beside, far, w, features, out, src, even, evenb, odd, *, side
):
    block = 2 * lax.axis_index("space") + lax.axis_index("wt")
    rows, width = center.shape
    conv(table, block, center, beside, far, w, src, even, odd, side)
    acc = conv_sum(even, evenb, odd, w, rows, width, side)
    total = jnp.maximum(features[...].astype(jnp.float32) + acc, 0.0)
    out[...] = total * occupancy[0, 0].astype(jnp.float32)


def params(flops=0, moved=0):
    return dict(
        compiler_params=pltpu.CompilerParams(vmem_limit_bytes=40 * 2**20),
        cost_estimate=pl.CostEstimate(
            flops=flops, bytes_accessed=moved, transcendentals=0
        ),
    )


def vmem(count):
    return [pl.BlockSpec(memory_space=VMEM)] * count


def smem(count):
    return [pl.BlockSpec(memory_space=SMEM)] * count


def body(features, occupancy, neighbours, kernel_one, kernel_two):
    side, width = features.shape[1], features.shape[4]
    rows = side**3
    total = lax.axis_size(AXES)
    halves = [(i, i ^ 1) for i in range(total)]
    cycle = [(i, i - 2) if i % 2 == 0 else (i, i + 2) for i in range(total)]
    cycle[0], cycle[-1] = (0, 1), (total - 1, total - 2)
    back = [(j, i) for i, j in cycle]
    surface = surface_rows(side)

    own = features.reshape(rows, width)
    face = pl.pallas_call(
        functools.partial(pack_kernel, side=side),
        out_shape=jax.ShapeDtypeStruct((surface, width), jnp.bfloat16),
        in_specs=vmem(1),
        out_specs=vmem(1)[0],
        scratch_shapes=[VMEM((len(pieces(width)), rows, LANES), jnp.float32)],
        **params(),
    )(own)
    info = jnp.concatenate([neighbours, occupancy[:, None]], axis=1)
    info_other = lax.ppermute(info, AXES, halves)
    other = lax.ppermute(own, AXES, halves)
    far = lax.ppermute(face, AXES, cycle)

    def weights(kernel):
        flat = kernel.reshape((27,) + kernel.shape[3:])
        swapped = lax.ppermute(flat, AXES, halves)
        return pl.pallas_call(
            weights_kernel,
            out_shape=jax.ShapeDtypeStruct((27, width, width), jnp.bfloat16),
            in_specs=vmem(2),
            out_specs=vmem(1)[0],
            **params(),
        )(flat, swapped)

    w_one, w_two = weights(kernel_one), weights(kernel_two)
    scratch = [
        VMEM((len(pieces(width)), 4 * rows, LANES), jnp.float32),
        VMEM((3, side + 2, (side + 2) * side, width), jnp.float32),
        VMEM((3, side + 2, (side + 2) * side, width), jnp.bfloat16),
        VMEM((3, side + 2, side * side, width), jnp.bfloat16),
    ]
    flops = 2 * rows * 27 * width * width
    hidden, hidden_face = pl.pallas_call(
        functools.partial(first_kernel, side=side),
        out_shape=(
            jax.ShapeDtypeStruct((rows, width), jnp.bfloat16),
            jax.ShapeDtypeStruct((surface, width), jnp.bfloat16),
        ),
        in_specs=smem(2) + vmem(4),
        out_specs=tuple(vmem(2)),
        scratch_shapes=scratch,
        **params(flops),
    )(info_other[:, :27], info_other[:, 27:], other, own, far, w_one)
    hidden_own = lax.ppermute(hidden, AXES, halves)
    hidden_far = lax.ppermute(hidden_face, AXES, back)
    out = pl.pallas_call(
        functools.partial(second_kernel, side=side),
        out_shape=jax.ShapeDtypeStruct((rows, width), jnp.float32),
        in_specs=smem(2) + vmem(5),
        out_specs=vmem(1)[0],
        scratch_shapes=scratch,
        **params(flops),
    )(neighbours, occupancy[:, None], hidden_own, hidden, hidden_far, w_two, own)
    return out.reshape((1, side, side, side, width))


def solution(mesh):
    return jax.shard_map(
        body,
        mesh=mesh,
        in_specs=(
            P(AXES, None, None, None, None),
            P(AXES),
            P(AXES, None),
            P(None, None, None, None, "wt"),
            P(None, None, None, None, "wt"),
        ),
        out_specs=P(AXES, None, None, None, None),
        check_vma=False,
    )
```

```python
import functools

import jax
import jax.numpy as jnp
from jax import lax
from jax.experimental import pallas as pl
from jax.experimental.pallas import tpu as pltpu
from jax.sharding import PartitionSpec as P

AXES = ("space", "wt")
VMEM = pltpu.VMEM
SMEM = pltpu.SMEM
LANES = 128
F32 = jnp.float32
BF16 = jnp.bfloat16


def pieces(width):
    return [
        (p, p * LANES, min(LANES, width - p * LANES)) for p in range(-(-width // LANES))
    ]


def fill(wide, base, value):
    rows, width = value.shape
    for p, lane, lanes in pieces(width):
        wide[p, pl.ds(base, rows), 0:lanes] = value[:, lane : lane + lanes]


def whole(wide, width):
    return jnp.concatenate([wide[p, :, 0:lanes] for p, _, lanes in pieces(width)], axis=1)


def surface_rows(side):
    return 2 * side * side + 4 * (side - 2) * side


def pack_surface(wide, out_ref, side, change=lambda value: value):
    plane = side * side
    inner = (side - 2) * side
    last = side - 1
    for p, lane, lanes in pieces(out_ref.shape[1]):
        ref = wide.at[p]

        def store(row, value):
            value = change(value[:, :lanes]).astype(BF16)
            out_ref[pl.ds(row, value.shape[0]), lane : lane + lanes] = value

        store(0, ref[pl.ds(0, plane), :])
        store(plane, ref[pl.ds(last * plane, plane), :])
        row = 2 * plane
        for y in (0, last):
            parts = [
                ref[pl.ds(x * plane + y * side, side), :] for x in range(1, last)
            ]
            store(row, jnp.concatenate(parts, axis=0))
            row += inner
        for z in (0, last):
            store(row, ref[pl.ds(plane + z, inner, stride=side), :])
            row += inner


def spread_surface(packed_ref, faces, slot, side):
    plane = side * side
    inner = (side - 2) * side
    last = side - 1
    base = slot * 6 * plane
    packed = packed_ref[...].astype(F32)
    for p, lane, lanes in pieces(packed.shape[1]):
        ref = faces.at[p]
        part = packed[:, lane : lane + lanes]
        if lanes < LANES:
            pad = jnp.zeros((part.shape[0], LANES - lanes), F32)
            part = jnp.concatenate([part, pad], axis=1)
        ref[pl.ds(base, 2 * plane), :] = part[: 2 * plane]
        row = 2 * plane
        for f in range(2, 6):
            ref[pl.ds(base + f * plane + side, inner), :] = part[row : row + inner]
            row += inner
        for end, x in ((0, 0), (1, last)):
            for f, y in ((2, 0), (3, last)):
                ref[pl.ds(base + f * plane + x * side, side), :] = ref[
                    pl.ds(base + end * plane + y * side, side), :
                ]
            for f, z in ((4, 0), (5, last)):
                ref[pl.ds(base + f * plane + x * side, side), :] = ref[
                    pl.ds(base + end * plane + z, side, stride=side), :
                ]


def pack_kernel(x_ref, out_ref, wide, *, side):
    fill(wide, 0, x_ref[...].astype(F32))
    pack_surface(wide, out_ref, side)


def weights_kernel(own_ref, other_ref, out_ref):
    core = lax.axis_index("wt")
    taps, depth, both = own_ref.shape
    width = out_ref.shape[2]
    half = depth * (both // width)
    for ref, place in ((own_ref, core), (other_ref, 1 - core)):
        for group in range(both // width):
            row = pl.multiple_of(place * half + group * depth, 16)
            out_ref[:, pl.ds(row, depth), :] = ref[
                :, :, group * width : (group + 1) * width
            ]


def shifts(middle, low, high, mask):
    side = middle.shape[1]
    return (
        pltpu.roll(jnp.where(mask == side - 1, low, middle), 1, axis=1),
        middle,
        pltpu.roll(jnp.where(mask == 0, high, middle), side - 1, axis=1),
    )


def inside_kernel(center, w, out, surface, wide, even, odd, *, side):
    rows, width = center.shape
    plane = side * side
    fill(wide, 0, center[...].astype(F32))
    pack_surface(wide, surface, side)
    mask = lax.broadcasted_iota(jnp.int32, (side, side, LANES), 1)
    nothing = jnp.zeros((side, side, LANES), F32)
    edge = jnp.zeros((3, side, side, width), BF16)
    even[:, :, 0:side, :] = edge
    even[:, :, side + plane : plane + 2 * side, :] = edge
    for p, lane, lanes in pieces(width):
        for x in range(side):
            middle = wide[p, pl.ds(x * plane, plane), :].reshape(side, side, LANES)
            for k, value in enumerate(shifts(middle, nothing, nothing, mask)):
                value = value.reshape(plane, LANES)[:, :lanes].astype(BF16)
                even[k, x, side : side + plane, lane : lane + lanes] = value
                odd[k, x, :, lane : lane + lanes] = value
    for i in (1, 0, 2):
        first, count = (1, 0, 0)[i], side - (i != 1)
        source = (0, 0, 1)[i]
        acc = jnp.zeros((count * plane, width), F32)
        for j in range(3):
            for k in range(3):
                if j == 1:
                    part = odd[k, source : source + count]
                else:
                    part = even[
                        k, source : source + count, j * side : j * side + plane
                    ]
                acc += jnp.dot(
                    part.reshape(count * plane, width),
                    w[9 * i + 3 * j + k],
                    preferred_element_type=F32,
                )
        if i == 1:
            out[...] = acc
        else:
            out[pl.ds(first * plane, count * plane), :] += acc


def add_outside(table, block, sources, inside, w, total, faces, even, odd, side):
    rows, width = inside.shape
    plane = side * side
    last = side - 1
    fill(faces, 0, jnp.zeros((6 * plane, width), F32))
    for slot, source in enumerate(sources):
        spread_surface(source, faces, slot + 1, side)
    pair = block + 1 - 2 * lax.rem(block, 2)

    def start(face, a, b, c, row):
        n = table[0, 9 * (a + 1) + 3 * (b + 1) + c + 1]
        near = jnp.where(n == block, 2, jnp.where(n == pair, 1, 3))
        slot = jnp.where(n < 0, 0, near)
        return pl.multiple_of((slot * 6 + face) * plane + row, side)

    mask = lax.broadcasted_iota(jnp.int32, (side, side, LANES), 1)
    for group in range(6):
        axis, up = divmod(group, 2)
        face = 2 * axis + 1 - up
        sign = 2 * up - 1
        for to, count, row, b in (
            (0, 1, last * side, -1),
            (1, side, 0, 0),
            (side + 1, 1, 0, 1),
        ):
            for p, lane, lanes in pieces(width):
                place = pl.ds(to * side, count * side)
                if axis > 0 and b != 0:
                    blank = jnp.zeros((3, side, lanes), BF16)
                    even[group, :, place, lane : lane + lanes] = blank
                    continue

                def chunk(c):
                    if axis == 2:
                        if c != 0:
                            return jnp.zeros((count, side, LANES), F32)
                        at = start(face, 0, 0, sign, row)
                    elif axis == 1:
                        at = start(face, 0, sign, c, row)
                    else:
                        at = start(face, sign, b, c, row)
                    value = faces[p, pl.ds(at, count * side), :]
                    return value.reshape(count, side, LANES)

                moved = shifts(chunk(0), chunk(-1), chunk(1), mask[:count])
                for k, value in enumerate(moved):
                    value = value.reshape(count * side, LANES)[:, :lanes]
                    if b == 0:
                        odd[group, k, :, lane : lane + lanes] = value.astype(BF16)
                    even[group, k, place, lane : lane + lanes] = value.astype(BF16)

    sums = [None] * 6
    for i in range(3):
        for j in range(3):
            for k in range(3):
                parts, groups = [], []
                for axis, tap, chunk, shift in ((0, i, j, k), (1, j, i, k), (2, k, i, j)):
                    if tap == 1:
                        continue
                    group = 2 * axis + tap // 2
                    if chunk == 1:
                        parts.append(odd[group, shift])
                    else:
                        parts.append(
                            even[group, shift, chunk * side : chunk * side + plane]
                        )
                    groups.append(group)
                if not parts:
                    continue
                product = jnp.dot(
                    jnp.concatenate(parts, axis=0),
                    w[9 * i + 3 * j + k],
                    preferred_element_type=F32,
                )
                for n, group in enumerate(groups):
                    part = product[n * plane : (n + 1) * plane]
                    sums[group] = part if sums[group] is None else sums[group] + part

    for p, lane, lanes in pieces(width):
        ref = total.at[p]
        part = [value[:, lane : lane + lanes] for value in sums]
        if lanes < LANES:
            pad = jnp.zeros((plane, LANES - lanes), F32)
            part = [jnp.concatenate([value, pad], axis=1) for value in part]
        ref[:, 0:lanes] = inside[:, lane : lane + lanes]
        for up, x in ((0, 0), (1, last)):
            ref[pl.ds(x * plane, plane), :] += part[up]
        for up, y in ((0, 0), (1, last)):
            for x in range(side):
                ref[pl.ds(x * plane + y * side, side), :] += part[2 + up][
                    x * side : (x + 1) * side
                ]
        for up, z in ((0, 0), (1, last)):
            ref[pl.ds(z, plane, stride=side), :] += part[4 + up]


def first_kernel(
    table, beside, center, far, inside, w, out, surface, total, faces, even, odd, *, side
):
    block = 2 * lax.axis_index("space") + 1 - lax.axis_index("wt")
    add_outside(
        table, block, (beside, center, far), inside, w, total, faces, even, odd, side
    )
    active = (table[0, 13] >= 0).astype(F32)

    def change(value):
        return jnp.maximum(value, 0.0) * active

    pack_surface(total, surface, side, change)
    out[...] = change(whole(total, out.shape[1])).astype(BF16)


def second_kernel(
    table,
    occupancy,
    beside,
    center,
    far,
    inside,
    w,
    features,
    out,
    total,
    faces,
    even,
    odd,
    *,
    side,
):
    block = 2 * lax.axis_index("space") + lax.axis_index("wt")
    add_outside(
        table, block, (beside, center, far), inside, w, total, faces, even, odd, side
    )
    value = features[...].astype(F32) + whole(total, out.shape[1])
    out[...] = jnp.maximum(value, 0.0) * occupancy[0].astype(F32)


def call(kernel, operands, outs, scratch=(), scalars=0, flops=0):
    outs = [jax.ShapeDtypeStruct(shape, kind) for shape, kind in outs]
    moved = sum(o.size * o.dtype.itemsize for o in list(operands) + outs)
    result = pl.pallas_call(
        kernel,
        out_shape=outs,
        in_specs=[pl.BlockSpec(memory_space=SMEM)] * scalars
        + [pl.BlockSpec(memory_space=VMEM)] * (len(operands) - scalars),
        out_specs=[pl.BlockSpec(memory_space=VMEM)] * len(outs),
        scratch_shapes=list(scratch),
        compiler_params=pltpu.CompilerParams(vmem_limit_bytes=32 * 2**20),
        cost_estimate=pl.CostEstimate(
            flops=flops, bytes_accessed=moved, transcendentals=0
        ),
    )(*operands)
    return result[0] if len(outs) == 1 else result


def body(features, occupancy, neighbours, kernel_one, kernel_two):
    side, width = features.shape[1], features.shape[4]
    rows, plane = side**3, side * side
    total = lax.axis_size(AXES)
    halves = [(i, i ^ 1) for i in range(total)]
    cycle = [(i, i - 2) if i % 2 == 0 else (i, i + 2) for i in range(total)]
    cycle[0], cycle[-1] = (0, 1), (total - 1, total - 2)
    back = [(j, i) for i, j in cycle]
    face = ((surface_rows(side), width), BF16)
    block = ((rows, width), BF16)
    wide = ((rows, width), F32)
    count = len(pieces(width))
    flops = 2 * rows * 27 * width * width

    own = features.reshape(rows, width)
    own_face = call(
        functools.partial(pack_kernel, side=side),
        (own,),
        [face],
        [VMEM((count, rows, LANES), F32)],
    )
    table_other = lax.ppermute(neighbours, AXES, halves)
    other = lax.ppermute(own, AXES, halves)
    far = lax.ppermute(own_face, AXES, cycle)

    def weights(kernel):
        flat = kernel.reshape((27,) + kernel.shape[3:])
        swapped = lax.ppermute(flat, AXES, halves)
        return call(weights_kernel, (flat, swapped), [((27, width, width), BF16)])

    w_one, w_two = weights(kernel_one), weights(kernel_two)

    def inside(center, w):
        return call(
            functools.partial(inside_kernel, side=side),
            (center, w),
            [wide, face],
            [
                VMEM((count, rows, LANES), F32),
                VMEM((3, side, plane + 2 * side, width), BF16),
                VMEM((3, side, plane, width), BF16),
            ],
            flops=flops,
        )

    outside = [
        VMEM((count, rows, LANES), F32),
        VMEM((count, 4 * 6 * plane, LANES), F32),
        VMEM((6, 3, plane + 2 * side, width), BF16),
        VMEM((6, 3, plane, width), BF16),
    ]
    inside_one, other_face = inside(other, w_one)
    hidden, hidden_face = call(
        functools.partial(first_kernel, side=side),
        (table_other, own_face, other_face, far, inside_one, w_one),
        [block, face],
        outside,
        scalars=1,
        flops=flops // 4,
    )
    hidden_own = lax.ppermute(hidden, AXES, halves)
    hidden_far = lax.ppermute(hidden_face, AXES, back)
    inside_two, hidden_own_face = inside(hidden_own, w_two)
    out = call(
        functools.partial(second_kernel, side=side),
        (
            neighbours,
            occupancy,
            hidden_face,
            hidden_own_face,
            hidden_far,
            inside_two,
            w_two,
            own,
        ),
        [wide],
        outside,
        scalars=2,
        flops=flops // 4,
    )
    return out.reshape((1, side, side, side, width))


def solution(mesh):
    return jax.shard_map(
        body,
        mesh=mesh,
        in_specs=(
            P(AXES, None, None, None, None),
            P(AXES),
            P(AXES, None),
            P(None, None, None, None, "wt"),
            P(None, None, None, None, "wt"),
        ),
        out_specs=P(AXES, None, None, None, None),
        check_vma=False,
    )
```

```python
import functools

import jax
import jax.numpy as jnp
from jax import lax
from jax.experimental import pallas as pl
from jax.experimental.pallas import tpu as pltpu
from jax.sharding import PartitionSpec as P

PARTS = 2
PACK_COST = 4 * 10**9
AXES = ("space", "wt")
VMEM = pltpu.VMEM
SMEM = pltpu.SMEM
LANES = 128
F32 = jnp.float32
BF16 = jnp.bfloat16


def pieces(width):
    return [
        (p, p * LANES, min(LANES, width - p * LANES)) for p in range(-(-width // LANES))
    ]


def fill(wide, base, value):
    rows, width = value.shape
    for p, lane, lanes in pieces(width):
        wide[p, pl.ds(base, rows), 0:lanes] = value[:, lane : lane + lanes]


def surface_rows(side):
    return 2 * side * side + 4 * (side - 2) * side


def pack_surface(wide, out_ref, side, change=lambda value: value):
    plane = side * side
    inner = (side - 2) * side
    last = side - 1
    for p, lane, lanes in pieces(out_ref.shape[1]):
        ref = wide.at[p]

        def store(row, value):
            value = change(value[:, :lanes]).astype(BF16)
            out_ref[pl.ds(row, value.shape[0]), lane : lane + lanes] = value

        store(0, ref[pl.ds(0, plane), :])
        store(plane, ref[pl.ds(last * plane, plane), :])
        row = 2 * plane
        for y in (0, last):
            parts = [
                ref[pl.ds(x * plane + y * side, side), :] for x in range(1, last)
            ]
            store(row, jnp.concatenate(parts, axis=0))
            row += inner
        for z in (0, last):
            store(row, ref[pl.ds(plane + z, inner, stride=side), :])
            row += inner


def spread_surface(packed_ref, faces, slot, side):
    plane = side * side
    inner = (side - 2) * side
    last = side - 1
    base = slot * 6 * plane
    packed = packed_ref[...].astype(F32)
    for p, lane, lanes in pieces(packed.shape[1]):
        ref = faces.at[p]
        part = packed[:, lane : lane + lanes]
        if lanes < LANES:
            pad = jnp.zeros((part.shape[0], LANES - lanes), F32)
            part = jnp.concatenate([part, pad], axis=1)
        ref[pl.ds(base, 2 * plane), :] = part[: 2 * plane]
        row = 2 * plane
        for f in range(2, 6):
            ref[pl.ds(base + f * plane + side, inner), :] = part[row : row + inner]
            row += inner
        for end, x in ((0, 0), (1, last)):
            for f, y in ((2, 0), (3, last)):
                ref[pl.ds(base + f * plane + x * side, side), :] = ref[
                    pl.ds(base + end * plane + y * side, side), :
                ]
            for f, z in ((4, 0), (5, last)):
                ref[pl.ds(base + f * plane + x * side, side), :] = ref[
                    pl.ds(base + end * plane + z, side, stride=side), :
                ]


def cut_surface(wide, faces, slot, side):
    plane = side * side
    last = side - 1
    base = slot * 6 * plane
    for p in range(wide.shape[0]):
        for n, x in enumerate((0, last)):
            faces[p, pl.ds(base + n * plane, plane), :] = wide[
                p, pl.ds(x * plane, plane), :
            ]
        for n, y in ((2, 0), (3, last)):
            for x in range(side):
                faces[p, pl.ds(base + n * plane + x * side, side), :] = wide[
                    p, pl.ds(x * plane + y * side, side), :
                ]
        for n, z in ((4, 0), (5, last)):
            faces[p, pl.ds(base + n * plane, plane), :] = wide.at[p][
                pl.ds(z, plane, stride=side), :
            ]


def pack_kernel(x_ref, out_ref, *refs, side):
    *pieces_out, wide = refs
    fill(wide, 0, x_ref[...].astype(F32))
    pack_surface(wide, out_ref, side)
    share(x_ref[...], pieces_out)


def share(value, refs):
    for n, ref in enumerate(refs):
        count = ref.shape[0]
        ref[...] = value[n * count : (n + 1) * count]


def weights_kernel(own_ref, other_ref, out_ref):
    core = lax.axis_index("wt")
    taps, depth, both = own_ref.shape
    width = out_ref.shape[2]
    half = depth * (both // width)
    for ref, place in ((own_ref, core), (other_ref, 1 - core)):
        for group in range(both // width):
            row = pl.multiple_of(place * half + group * depth, 16)
            out_ref[:, pl.ds(row, depth), :] = ref[
                :, :, group * width : (group + 1) * width
            ]


def shifts(middle, low, high, mask):
    side = middle.shape[1]
    return (
        pltpu.roll(jnp.where(mask == side - 1, low, middle), 1, axis=1),
        middle,
        pltpu.roll(jnp.where(mask == 0, high, middle), side - 1, axis=1),
    )


def inside_kernel(*refs, side, block_of):
    table, beside, *centers, w, total, near, masks, wide, faces, even, odd = refs
    width = w.shape[2]
    rows, plane = total.shape[1], side * side
    for n, part in enumerate(centers):
        fill(wide, n * part.shape[0], part[...].astype(F32))
    fill(faces, 0, jnp.zeros((6 * plane, width), F32))
    spread_surface(beside, faces, 1, side)
    cut_surface(wide, faces, 2, side)
    choose_near(table, block_of(), faces, near, masks, side)
    mask = lax.broadcasted_iota(jnp.int32, (side, side, LANES), 1)
    nothing = jnp.zeros((side, side, LANES), F32)
    edge = jnp.zeros((3, side, side, width), BF16)
    even[:, :, 0:side, :] = edge
    even[:, :, side + plane : plane + 2 * side, :] = edge
    for p, lane, lanes in pieces(width):
        for x in range(side):
            middle = wide[p, pl.ds(x * plane, plane), :].reshape(side, side, LANES)
            for k, value in enumerate(shifts(middle, nothing, nothing, mask)):
                value = value.reshape(plane, LANES)[:, :lanes].astype(BF16)
                even[k, x, side : side + plane, lane : lane + lanes] = value
                odd[k, x, :, lane : lane + lanes] = value
    for i in (1, 0, 2):
        first, count = (1, 0, 0)[i], side - (i != 1)
        source = (0, 0, 1)[i]
        acc = jnp.zeros((count * plane, width), F32)
        for j in range(3):
            for k in range(3):
                if j == 1:
                    part = odd[k, source : source + count]
                else:
                    part = even[
                        k, source : source + count, j * side : j * side + plane
                    ]
                acc += jnp.dot(
                    part.reshape(count * plane, width),
                    w[9 * i + 3 * j + k],
                    preferred_element_type=F32,
                )
        for p, lane, lanes in pieces(width):
            part = acc[:, lane : lane + lanes]
            place = pl.ds(first * plane, count * plane)
            if i == 1:
                total[p, place, 0:lanes] = part
            else:
                total[p, place, 0:lanes] += part


def borders(side):
    last = side - 1
    for group in range(6):
        axis, up = divmod(group, 2)
        face = 2 * axis + 1 - up
        sign = 2 * up - 1
        for to, count, row, b in (
            (0, 1, last * side, -1),
            (1, side, 0, 0),
            (side + 1, 1, 0, 1),
        ):
            offsets = {}
            for c in (-1, 0, 1):
                if axis == 0:
                    offsets[c] = (sign, b, c)
                elif axis == 1 and b == 0:
                    offsets[c] = (0, sign, c)
                elif axis == 2 and b == 0 and c == 0:
                    offsets[c] = (0, 0, sign)
            yield group, to, count, row, face, offsets


def entry(offset):
    a, b, c = offset
    return 9 * (a + 1) + 3 * (b + 1) + c + 1


def choose_near(table, block, faces, near, masks, side):
    plane = side * side
    pair = block + 1 - 2 * lax.rem(block, 2)

    def slot(n):
        return jnp.where(n < 0, 0, jnp.where(n == block, 2, jnp.where(n == pair, 1, 3)))

    slots = [slot(table[0, t]) for t in range(27)]
    for t, value in enumerate(slots):
        flag = (value > 0 if t == 13 else value == 3).astype(F32)
        masks[pl.ds(8 * t, 8), :] = jnp.full((8, LANES), flag, F32)
    for group, to, count, row, face, offsets in borders(side):
        for c, offset in offsets.items():
            value = slots[entry(offset)]
            source = jnp.where(value == 3, 0, value)
            start = pl.multiple_of((source * 6 + face) * plane + row, side)
            place = pl.ds(((3 * group + c + 1) * (side + 2) + to) * side, count * side)
            for p in range(faces.shape[0]):
                near[p, place, :] = faces[p, pl.ds(start, count * side), :]


def add_outside(far, w, near, masks, total, faces, even, odd, side):
    width = w.shape[2]
    plane = side * side
    last = side - 1
    spread_surface(far, faces, 0, side)
    mask = lax.broadcasted_iota(jnp.int32, (side, side, LANES), 1)
    for group, to, count, row, face, offsets in borders(side):
        for p, lane, lanes in pieces(width):
            place = pl.ds(to * side, count * side)
            if not offsets:
                blank = jnp.zeros((3, side, lanes), BF16)
                even[group, :, place, lane : lane + lanes] = blank
                continue

            def chunk(c):
                if c not in offsets:
                    return jnp.zeros((count, side, LANES), F32)
                away = masks[pl.ds(8 * entry(offsets[c]), 8), :] > 0
                at = ((3 * group + c + 1) * (side + 2) + to) * side
                afar = faces[p, pl.ds(face * plane + row, count * side), :]
                here = near[p, pl.ds(at, count * side), :]
                shape = (count, side, LANES)
                return jnp.where(
                    jnp.broadcast_to(away[None], shape),
                    afar.reshape(shape),
                    here.reshape(shape),
                )

            moved = shifts(chunk(0), chunk(-1), chunk(1), mask[:count])
            for k, value in enumerate(moved):
                value = value.reshape(count * side, LANES)[:, :lanes]
                if count == side:
                    odd[group, k, :, lane : lane + lanes] = value.astype(BF16)
                even[group, k, place, lane : lane + lanes] = value.astype(BF16)

    sums = [None] * 6
    for i in range(3):
        for j in range(3):
            for k in range(3):
                parts, groups = [], []
                for axis, tap, chunk, shift in ((0, i, j, k), (1, j, i, k), (2, k, i, j)):
                    if tap == 1:
                        continue
                    group = 2 * axis + tap // 2
                    if chunk == 1:
                        parts.append(odd[group, shift])
                    else:
                        parts.append(
                            even[group, shift, chunk * side : chunk * side + plane]
                        )
                    groups.append(group)
                if not parts:
                    continue
                product = jnp.dot(
                    jnp.concatenate(parts, axis=0),
                    w[9 * i + 3 * j + k],
                    preferred_element_type=F32,
                )
                for n, group in enumerate(groups):
                    part = product[n * plane : (n + 1) * plane]
                    sums[group] = part if sums[group] is None else sums[group] + part

    for p, lane, lanes in pieces(width):
        ref = total.at[p]
        part = [value[:, lane : lane + lanes] for value in sums]
        if lanes < LANES:
            pad = jnp.zeros((plane, LANES - lanes), F32)
            part = [jnp.concatenate([value, pad], axis=1) for value in part]
        for up, x in ((0, 0), (1, last)):
            ref[pl.ds(x * plane, plane), :] += part[up]
        for up, y in ((0, 0), (1, last)):
            for x in range(side):
                ref[pl.ds(x * plane + y * side, side), :] += part[2 + up][
                    x * side : (x + 1) * side
                ]
        for up, z in ((0, 0), (1, last)):
            ref[pl.ds(z, plane, stride=side), :] += part[4 + up]


def first_kernel(far, w, total_in, near, masks, surface, *refs, side):
    *outs, total, faces, even, odd = refs
    add_outside(far, w, near, masks, total, faces, even, odd, side)
    active = masks[pl.ds(8 * 13, 1), :]

    def change(value):
        return jnp.maximum(value, 0.0) * active[:, : value.shape[1]]

    pack_surface(total, surface, side, change)
    for p, lane, lanes in pieces(w.shape[2]):
        for n, out in enumerate(outs):
            count = out.shape[0]
            value = change(total[p, pl.ds(n * count, count), 0:lanes])
            out[:, lane : lane + lanes] = value.astype(BF16)


def second_kernel(
    occupancy, far, w, features, total_in, near, masks, out, total, faces, even, odd, *, side
):
    add_outside(far, w, near, masks, total, faces, even, odd, side)
    active = occupancy[...].astype(F32)
    for p, lane, lanes in pieces(w.shape[2]):
        value = features[:, lane : lane + lanes].astype(F32) + total[p, :, 0:lanes]
        out[:, lane : lane + lanes] = jnp.maximum(value, 0.0) * active


def first_block():
    return 2 * lax.axis_index("space") + 1 - lax.axis_index("wt")


def second_block():
    return 2 * lax.axis_index("space") + lax.axis_index("wt")


def call(kernel, operands, outs, scratch=(), scalars=0, cost=0, aliases={}):
    outs = [jax.ShapeDtypeStruct(shape, kind) for shape, kind in outs]
    result = pl.pallas_call(
        kernel,
        out_shape=outs,
        in_specs=[pl.BlockSpec(memory_space=SMEM)] * scalars
        + [pl.BlockSpec(memory_space=VMEM)] * (len(operands) - scalars),
        out_specs=[pl.BlockSpec(memory_space=VMEM)] * len(outs),
        scratch_shapes=list(scratch),
        input_output_aliases=aliases,
        compiler_params=pltpu.CompilerParams(vmem_limit_bytes=32 * 2**20),
        cost_estimate=pl.CostEstimate(flops=cost, bytes_accessed=0, transcendentals=0),
    )(*operands)
    return result[0] if len(outs) == 1 else result


def body(features, occupancy, neighbours, kernel_one, kernel_two):
    side, width = features.shape[1], features.shape[4]
    rows, plane = side**3, side * side
    total = lax.axis_size(AXES)
    halves = [(i, i ^ 1) for i in range(total)]
    cycle = [(i, i - 2) if i % 2 == 0 else (i, i + 2) for i in range(total)]
    cycle[0], cycle[-1] = (0, 1), (total - 1, total - 2)
    back = [(j, i) for i, j in cycle]
    face = ((surface_rows(side), width), BF16)
    piece = ((rows // PARTS, width), BF16)
    wide = ((rows, width), F32)
    count = len(pieces(width))

    own = features.reshape(rows, width)
    own_face, *own_parts = call(
        functools.partial(pack_kernel, side=side),
        (own,),
        [face] + [piece] * PARTS,
        [VMEM((count, rows, LANES), F32)],
        cost=PACK_COST,
    )
    table_other = lax.ppermute(neighbours, AXES, halves)
    other = [lax.ppermute(part, AXES, halves) for part in own_parts]
    far = lax.ppermute(own_face, AXES, cycle)

    def weights(kernel):
        flat = kernel.reshape((27,) + kernel.shape[3:])
        swapped = lax.ppermute(flat, AXES, halves)
        return call(weights_kernel, (flat, swapped), [((27, width, width), BF16)])

    w_one, w_two = weights(kernel_one), weights(kernel_two)

    sums = ((count, rows, LANES), F32)
    near = ((count, 6 * 3 * (side + 2) * side, LANES), F32)
    masks = ((27 * 8, LANES), F32)

    def inside(block_of, table, beside, center, w):
        return call(
            functools.partial(inside_kernel, side=side, block_of=block_of),
            (table, beside, *center, w),
            [sums, near, masks],
            [
                VMEM((count, rows, LANES), F32),
                VMEM((count, 3 * 6 * plane, LANES), F32),
                VMEM((3, side, plane + 2 * side, width), BF16),
                VMEM((3, side, plane, width), BF16),
            ],
            scalars=1,
        )

    planes = [
        VMEM((count, 6 * plane, LANES), F32),
        VMEM((6, 3, plane + 2 * side, width), BF16),
        VMEM((6, 3, plane, width), BF16),
    ]
    hidden_face, *hidden, _ = call(
        functools.partial(first_kernel, side=side),
        (far, w_one, *inside(first_block, table_other, own_face, other, w_one)),
        [face] + [piece] * PARTS + [sums],
        planes,
        aliases={2: 1 + PARTS},
    )
    hidden_own = [lax.ppermute(part, AXES, halves) for part in hidden]
    hidden_far = lax.ppermute(hidden_face, AXES, back)
    out, _ = call(
        functools.partial(second_kernel, side=side),
        (
            occupancy.reshape(1, 1),
            hidden_far,
            w_two,
            own,
            *inside(second_block, neighbours, hidden_face, hidden_own, w_two),
        ),
        [wide, sums],
        planes,
        aliases={4: 1},
    )
    return out.reshape((1, side, side, side, width))


def solution(mesh):
    return jax.shard_map(
        body,
        mesh=mesh,
        in_specs=(
            P(AXES, None, None, None, None),
            P(AXES),
            P(AXES, None),
            P(None, None, None, None, "wt"),
            P(None, None, None, None, "wt"),
        ),
        out_specs=P(AXES, None, None, None, None),
        check_vma=False,
    )
```

```python
import functools

import jax
import jax.numpy as jnp
from jax import lax
from jax.experimental import pallas as pl
from jax.experimental.pallas import tpu as pltpu
from jax.sharding import PartitionSpec as P

PARTS = 2
PACK_COST = 4 * 10**9
AXES = ("space", "wt")
VMEM = pltpu.VMEM
SMEM = pltpu.SMEM
LANES = 128
F32 = jnp.float32
BF16 = jnp.bfloat16


def pieces(width):
    return [
        (p, p * LANES, min(LANES, width - p * LANES)) for p in range(-(-width // LANES))
    ]


def fill(wide, base, value):
    rows, width = value.shape
    for p, lane, lanes in pieces(width):
        wide[p, pl.ds(base, rows), 0:lanes] = value[:, lane : lane + lanes]


def surface_rows(side):
    return 2 * side * side + 4 * (side - 2) * side


def folded_rows(side, width):
    return -(-surface_rows(side) * width // LANES)


def pack_surface(wide, out_ref, side, width, change=lambda value: value):
    plane = side * side
    inner = (side - 2) * side
    last = side - 1
    rows = surface_rows(side)
    for p, lane, lanes in pieces(width):
        ref = wide.at[p]
        parts = [ref[pl.ds(0, plane), :], ref[pl.ds(last * plane, plane), :]]
        for y in (0, last):
            for x in range(1, last):
                parts.append(ref[pl.ds(x * plane + y * side, side), :])
        for z in (0, last):
            parts.append(ref[pl.ds(plane + z, inner, stride=side), :])
        value = change(jnp.concatenate(parts, axis=0))
        folds = LANES // lanes
        count = rows // folds
        result = value[:count]
        position = lax.broadcasted_iota(jnp.int32, (count, LANES), 1)
        for n in range(1, folds):
            part = pltpu.roll(value[n * count : (n + 1) * count], n * lanes, axis=1)
            result = jnp.where(position >= n * lanes, part, result)
        out_ref[pl.ds(p * rows, count), :] = result.astype(BF16)


def spread_surface(packed_ref, faces, slot, side, width):
    plane = side * side
    inner = (side - 2) * side
    last = side - 1
    base = slot * 6 * plane
    rows = surface_rows(side)
    for p, lane, lanes in pieces(width):
        ref = faces.at[p]
        folds = LANES // lanes
        part = packed_ref[pl.ds(p * rows, rows // folds), :].astype(F32)
        if folds > 1:
            turned = [part] + [
                pltpu.roll(part, LANES - n * lanes, axis=1) for n in range(1, folds)
            ]
            part = jnp.concatenate(turned, axis=0)
        ref[pl.ds(base, 2 * plane), :] = part[: 2 * plane]
        row = 2 * plane
        for f in range(2, 6):
            ref[pl.ds(base + f * plane + side, inner), :] = part[row : row + inner]
            row += inner
        for end, x in ((0, 0), (1, last)):
            for f, y in ((2, 0), (3, last)):
                ref[pl.ds(base + f * plane + x * side, side), :] = ref[
                    pl.ds(base + end * plane + y * side, side), :
                ]
            for f, z in ((4, 0), (5, last)):
                ref[pl.ds(base + f * plane + x * side, side), :] = ref[
                    pl.ds(base + end * plane + z, side, stride=side), :
                ]


def cut_surface(wide, faces, slot, side):
    plane = side * side
    last = side - 1
    base = slot * 6 * plane
    for p in range(wide.shape[0]):
        for n, x in enumerate((0, last)):
            faces[p, pl.ds(base + n * plane, plane), :] = wide[
                p, pl.ds(x * plane, plane), :
            ]
        for n, y in ((2, 0), (3, last)):
            for x in range(side):
                faces[p, pl.ds(base + n * plane + x * side, side), :] = wide[
                    p, pl.ds(x * plane + y * side, side), :
                ]
        for n, z in ((4, 0), (5, last)):
            faces[p, pl.ds(base + n * plane, plane), :] = wide.at[p][
                pl.ds(z, plane, stride=side), :
            ]


def pack_kernel(x_ref, out_ref, *refs, side):
    *pieces_out, wide = refs
    fill(wide, 0, x_ref[...].astype(F32))
    pack_surface(wide, out_ref, side, x_ref.shape[1])
    share(x_ref[...], pieces_out)


def share(value, refs):
    for n, ref in enumerate(refs):
        count = ref.shape[0]
        ref[...] = value[n * count : (n + 1) * count]


def weight_rows(width, tap):
    return [
        (lane, 9 * lane + tap * lanes, lanes) for _, lane, lanes in pieces(width)
    ]


def weights_kernel(own_ref, other_ref, out_ref):
    core = lax.axis_index("wt")
    taps, depth, both = own_ref.shape
    width = out_ref.shape[2]
    half = depth * (both // width)
    step = 16
    for tap in range(taps):
        rows = {}
        for channel, row, count in weight_rows(width, tap % 9):
            for n in range(0, count, step):
                rows[channel + n] = row + n
        for ref, place in ((own_ref, core), (other_ref, 1 - core)):
            for group in range(both // width):
                lane = group * width
                value = ref[tap, :, lane : lane + width]
                for n in range(0, depth, step):
                    at = group * depth + n
                    row = jnp.where(place == 0, rows[at], rows[at + half])
                    row = pl.multiple_of(row, step)
                    out_ref[tap // 9, pl.ds(row, step), :] = value[n : n + step]


def tap_weights(w, tap):
    third, tap = divmod(tap, 9)
    return jnp.concatenate(
        [w[third, pl.ds(row, count), :] for _, row, count in weight_rows(w.shape[2], tap)],
        axis=0,
    )


def shifts(middle, low, high, mask):
    side = middle.shape[1]
    return (
        pltpu.roll(jnp.where(mask == side - 1, low, middle), 1, axis=1),
        middle,
        pltpu.roll(jnp.where(mask == 0, high, middle), side - 1, axis=1),
    )


def inside_kernel(*refs, side, block_of):
    table_ref, beside, *centers, w, total, near, masks = refs[:-5]
    wide, faces, lhs, table, semaphore = refs[-5:]
    copy = pltpu.make_async_copy(table_ref, table, semaphore)
    copy.start()
    width = w.shape[2]
    plane = side * side
    for n, part in enumerate(centers):
        fill(wide, n * part.shape[0], part[...].astype(F32))
    mask = lax.broadcasted_iota(jnp.int32, (side, side, LANES), 1)
    nothing = jnp.zeros((side, side, LANES), F32)
    edge = jnp.zeros((1, side, LANES), F32)
    for p, lane, lanes in pieces(width):
        folds = LANES // lanes
        for x in range(side):
            middle = wide[p, pl.ds(x * plane, plane), :].reshape(side, side, LANES)
            if folds > 1:
                position = lax.broadcasted_iota(jnp.int32, middle.shape, 2)
                for n in range(1, folds):
                    turned = pltpu.roll(middle, n * lanes, axis=2)
                    middle = jnp.where(position >= n * lanes, turned, middle)
            moved = shifts(middle, nothing, nothing, mask)
            taps = []
            for j in range(3):
                for k in range(3):
                    value = moved[k]
                    if j == 0:
                        value = jnp.concatenate([edge, value[: side - 1]], axis=0)
                    elif j == 2:
                        value = jnp.concatenate([value[1:], edge], axis=0)
                    taps.append(value.reshape(plane, LANES))
            for t in range(0, 9, folds):
                value = taps[t]
                used = min(folds, 9 - t)
                for n in range(1, used):
                    position = lax.broadcasted_iota(jnp.int32, value.shape, 1)
                    value = jnp.where(position >= n * lanes, taps[t + n], value)
                at = 9 * lane + t * lanes
                lhs[pl.ds(x * plane, plane), at : at + used * lanes] = value[
                    :, : used * lanes
                ].astype(BF16)
    for i in (1, 0, 2):
        first, source, count = (1, 0, 0)[i], (0, 0, 1)[i], side - (i != 1)
        acc = jnp.dot(
            lhs[pl.ds(source * plane, count * plane), :],
            w[i],
            preferred_element_type=F32,
        )
        for p, lane, lanes in pieces(width):
            part = acc[:, lane : lane + lanes]
            place = pl.ds(first * plane, count * plane)
            if i == 1:
                total[p, place, 0:lanes] = part
            else:
                total[p, place, 0:lanes] += part
    fill(faces, 0, jnp.zeros((6 * plane, width), F32))
    spread_surface(beside, faces, 1, side, width)
    cut_surface(wide, faces, 2, side)
    copy.wait()
    choose_near(table, block_of(), faces, near, masks, side)


def borders(side):
    last = side - 1
    for group in range(6):
        axis, up = divmod(group, 2)
        face = 2 * axis + 1 - up
        sign = 2 * up - 1
        for to, count, row, b in (
            (0, 1, last * side, -1),
            (1, side, 0, 0),
            (side + 1, 1, 0, 1),
        ):
            offsets = {}
            for c in (-1, 0, 1):
                if axis == 0:
                    offsets[c] = (sign, b, c)
                elif axis == 1 and b == 0:
                    offsets[c] = (0, sign, c)
                elif axis == 2 and b == 0 and c == 0:
                    offsets[c] = (0, 0, sign)
            yield group, to, count, row, face, offsets


def entry(offset):
    a, b, c = offset
    return 9 * (a + 1) + 3 * (b + 1) + c + 1


def choose_near(table, block, faces, near, masks, side):
    plane = side * side
    pair = block + 1 - 2 * lax.rem(block, 2)

    def slot(n):
        return jnp.where(n < 0, 0, jnp.where(n == block, 2, jnp.where(n == pair, 1, 3)))

    slots = [slot(table[0, t]) for t in range(27)]
    for t, value in enumerate(slots):
        flag = (value > 0 if t == 13 else value == 3).astype(F32)
        masks[pl.ds(8 * t, 8), :] = jnp.full((8, LANES), flag, F32)
    for group, to, count, row, face, offsets in borders(side):
        for c, offset in offsets.items():
            value = slots[entry(offset)]
            source = jnp.where(value == 3, 0, value)
            start = pl.multiple_of((source * 6 + face) * plane + row, side)
            place = pl.ds(((3 * group + c + 1) * (side + 2) + to) * side, count * side)
            for p in range(faces.shape[0]):
                near[p, place, :] = faces[p, pl.ds(start, count * side), :]


def add_outside(far, w, near, masks, total, faces, even, odd, side):
    width = w.shape[2]
    plane = side * side
    last = side - 1
    spread_surface(far, faces, 0, side, width)
    mask = lax.broadcasted_iota(jnp.int32, (side, side, LANES), 1)
    for group, to, count, row, face, offsets in borders(side):
        for p, lane, lanes in pieces(width):
            place = pl.ds(to * side, count * side)
            if not offsets:
                blank = jnp.zeros((3, side, lanes), BF16)
                even[group, :, place, lane : lane + lanes] = blank
                continue

            def chunk(c):
                if c not in offsets:
                    return jnp.zeros((count, side, LANES), F32)
                away = masks[pl.ds(8 * entry(offsets[c]), 8), :] > 0
                at = ((3 * group + c + 1) * (side + 2) + to) * side
                afar = faces[p, pl.ds(face * plane + row, count * side), :]
                here = near[p, pl.ds(at, count * side), :]
                shape = (count, side, LANES)
                return jnp.where(
                    jnp.broadcast_to(away[None], shape),
                    afar.reshape(shape),
                    here.reshape(shape),
                )

            moved = shifts(chunk(0), chunk(-1), chunk(1), mask[:count])
            for k, value in enumerate(moved):
                value = value.reshape(count * side, LANES)[:, :lanes]
                if count == side:
                    odd[group, k, :, lane : lane + lanes] = value.astype(BF16)
                even[group, k, place, lane : lane + lanes] = value.astype(BF16)

    sums = [None] * 6
    for i in range(3):
        for j in range(3):
            for k in range(3):
                parts, groups = [], []
                for axis, tap, chunk, shift in ((0, i, j, k), (1, j, i, k), (2, k, i, j)):
                    if tap == 1:
                        continue
                    group = 2 * axis + tap // 2
                    if chunk == 1:
                        parts.append(odd[group, shift])
                    else:
                        parts.append(
                            even[group, shift, chunk * side : chunk * side + plane]
                        )
                    groups.append(group)
                if not parts:
                    continue
                product = jnp.dot(
                    jnp.concatenate(parts, axis=0),
                    tap_weights(w, 9 * i + 3 * j + k),
                    preferred_element_type=F32,
                )
                for n, group in enumerate(groups):
                    part = product[n * plane : (n + 1) * plane]
                    sums[group] = part if sums[group] is None else sums[group] + part

    for p, lane, lanes in pieces(width):
        ref = total.at[p]
        part = [value[:, lane : lane + lanes] for value in sums]
        if lanes < LANES:
            pad = jnp.zeros((plane, LANES - lanes), F32)
            part = [jnp.concatenate([value, pad], axis=1) for value in part]
        for up, x in ((0, 0), (1, last)):
            ref[pl.ds(x * plane, plane), :] += part[up]
        for up, y in ((0, 0), (1, last)):
            for x in range(side):
                ref[pl.ds(x * plane + y * side, side), :] += part[2 + up][
                    x * side : (x + 1) * side
                ]
        for up, z in ((0, 0), (1, last)):
            ref[pl.ds(z, plane, stride=side), :] += part[4 + up]


def first_kernel(far, w, total_in, near, masks, surface, *refs, side):
    *outs, total, faces, even, odd = refs
    add_outside(far, w, near, masks, total, faces, even, odd, side)
    active = masks[pl.ds(8 * 13, 1), :]

    def change(value):
        return jnp.maximum(value, 0.0) * active[:, : value.shape[1]]

    pack_surface(total, surface, side, w.shape[2], change)
    for p, lane, lanes in pieces(w.shape[2]):
        for n, out in enumerate(outs):
            count = out.shape[0]
            value = change(total[p, pl.ds(n * count, count), 0:lanes])
            out[:, lane : lane + lanes] = value.astype(BF16)


def second_kernel(
    occupancy, far, w, features, total_in, near, masks, out, total, faces, even, odd, *, side
):
    add_outside(far, w, near, masks, total, faces, even, odd, side)
    active = occupancy[...].astype(F32)
    for p, lane, lanes in pieces(w.shape[2]):
        value = features[:, lane : lane + lanes].astype(F32) + total[p, :, 0:lanes]
        out[:, lane : lane + lanes] = jnp.maximum(value, 0.0) * active


def first_block():
    return 2 * lax.axis_index("space") + 1 - lax.axis_index("wt")


def second_block():
    return 2 * lax.axis_index("space") + lax.axis_index("wt")


def call(kernel, operands, outs, scratch=(), anywhere=0, cost=0, aliases={}):
    outs = [jax.ShapeDtypeStruct(shape, kind) for shape, kind in outs]
    result = pl.pallas_call(
        kernel,
        out_shape=outs,
        in_specs=[pl.BlockSpec(memory_space=pl.ANY)] * anywhere
        + [pl.BlockSpec(memory_space=VMEM)] * (len(operands) - anywhere),
        out_specs=[pl.BlockSpec(memory_space=VMEM)] * len(outs),
        scratch_shapes=list(scratch),
        input_output_aliases=aliases,
        compiler_params=pltpu.CompilerParams(vmem_limit_bytes=32 * 2**20),
        cost_estimate=pl.CostEstimate(flops=cost, bytes_accessed=0, transcendentals=0),
    )(*operands)
    return result[0] if len(outs) == 1 else result


def body(features, occupancy, neighbours, kernel_one, kernel_two):
    side, width = features.shape[1], features.shape[4]
    rows, plane = side**3, side * side
    total = lax.axis_size(AXES)
    halves = [(i, i ^ 1) for i in range(total)]
    cycle = [(i, i - 2) if i % 2 == 0 else (i, i + 2) for i in range(total)]
    cycle[0], cycle[-1] = (0, 1), (total - 1, total - 2)
    back = [(j, i) for i, j in cycle]
    face = ((folded_rows(side, width), LANES), BF16)
    piece = ((rows // PARTS, width), BF16)
    wide = ((rows, width), F32)
    count = len(pieces(width))

    own = features.reshape(rows, width)
    own_face, *own_parts = call(
        functools.partial(pack_kernel, side=side),
        (own,),
        [face] + [piece] * PARTS,
        [VMEM((count, rows, LANES), F32)],
        cost=PACK_COST,
    )
    table_other = lax.ppermute(neighbours, AXES, halves)
    other = [lax.ppermute(part, AXES, halves) for part in own_parts]
    far = lax.ppermute(own_face, AXES, cycle)

    def weights(kernel):
        flat = kernel.reshape((27,) + kernel.shape[3:])
        swapped = lax.ppermute(flat, AXES, halves)
        return call(weights_kernel, (flat, swapped), [((3, 9 * width, width), BF16)])

    w_one, w_two = weights(kernel_one), weights(kernel_two)

    sums = ((count, rows, LANES), F32)
    near = ((count, 6 * 3 * (side + 2) * side, LANES), F32)
    masks = ((27 * 8, LANES), F32)

    def inside(block_of, table, beside, center, w):
        return call(
            functools.partial(inside_kernel, side=side, block_of=block_of),
            (table, beside, *center, w),
            [sums, near, masks],
            [
                VMEM((count, rows, LANES), F32),
                VMEM((count, 3 * 6 * plane, LANES), F32),
                VMEM((rows, 9 * width), BF16),
                SMEM(table.shape, jnp.int32),
                pltpu.SemaphoreType.DMA,
            ],
            anywhere=1,
        )

    planes = [
        VMEM((count, 6 * plane, LANES), F32),
        VMEM((6, 3, plane + 2 * side, width), BF16),
        VMEM((6, 3, plane, width), BF16),
    ]
    hidden_face, *hidden, _ = call(
        functools.partial(first_kernel, side=side),
        (far, w_one, *inside(first_block, table_other, own_face, other, w_one)),
        [face] + [piece] * PARTS + [sums],
        planes,
        aliases={2: 1 + PARTS},
    )
    hidden_own = [lax.ppermute(part, AXES, halves) for part in hidden]
    hidden_far = lax.ppermute(hidden_face, AXES, back)
    out, _ = call(
        functools.partial(second_kernel, side=side),
        (
            occupancy.reshape(1, 1),
            hidden_far,
            w_two,
            own,
            *inside(second_block, neighbours, hidden_face, hidden_own, w_two),
        ),
        [wide, sums],
        planes,
        aliases={4: 1},
    )
    return out.reshape((1, side, side, side, width))


def solution(mesh):
    return jax.shard_map(
        body,
        mesh=mesh,
        in_specs=(
            P(AXES, None, None, None, None),
            P(AXES),
            P(AXES, None),
            P(None, None, None, None, "wt"),
            P(None, None, None, None, "wt"),
        ),
        out_specs=P(AXES, None, None, None, None),
        check_vma=False,
    )
```

```python
import functools

import jax
import jax.numpy as jnp
from jax import lax
from jax.experimental import pallas as pl
from jax.experimental.pallas import tpu as pltpu
from jax.sharding import PartitionSpec as P

PARTS = 2
PACK_COST = 4 * 10**9
FIRST_COST = 18 * 10**9
AXES = ("space", "wt")
VMEM = pltpu.VMEM
SMEM = pltpu.SMEM
LANES = 128
F32 = jnp.float32
BF16 = jnp.bfloat16


def pieces(width):
    return [
        (p, p * LANES, min(LANES, width - p * LANES)) for p in range(-(-width // LANES))
    ]


def fill(wide, base, value):
    rows, width = value.shape
    for p, lane, lanes in pieces(width):
        wide[p, pl.ds(base, rows), 0:lanes] = value[:, lane : lane + lanes]


def surface_rows(side):
    return 2 * side * side + 4 * (side - 2) * side


def folded_rows(side, width):
    return -(-surface_rows(side) * width // LANES)


def pack_surface(wide, out_ref, side, width, change=lambda value: value):
    plane = side * side
    inner = (side - 2) * side
    last = side - 1
    rows = surface_rows(side)
    for p, lane, lanes in pieces(width):
        ref = wide.at[p]
        parts = [ref[pl.ds(0, plane), :], ref[pl.ds(last * plane, plane), :]]
        for y in (0, last):
            for x in range(1, last):
                parts.append(ref[pl.ds(x * plane + y * side, side), :])
        for z in (0, last):
            parts.append(ref[pl.ds(plane + z, inner, stride=side), :])
        value = change(jnp.concatenate(parts, axis=0))
        folds = LANES // lanes
        count = rows // folds
        result = value[:count]
        position = lax.broadcasted_iota(jnp.int32, (count, LANES), 1)
        for n in range(1, folds):
            part = pltpu.roll(value[n * count : (n + 1) * count], n * lanes, axis=1)
            result = jnp.where(position >= n * lanes, part, result)
        out_ref[pl.ds(p * rows, count), :] = result.astype(BF16)


def spread_surface(packed_ref, faces, slot, side, width):
    plane = side * side
    inner = (side - 2) * side
    last = side - 1
    base = slot * 6 * plane
    rows = surface_rows(side)
    for p, lane, lanes in pieces(width):
        ref = faces.at[p]
        folds = LANES // lanes
        part = packed_ref[pl.ds(p * rows, rows // folds), :].astype(F32)
        if folds > 1:
            turned = [part] + [
                pltpu.roll(part, LANES - n * lanes, axis=1) for n in range(1, folds)
            ]
            part = jnp.concatenate(turned, axis=0)
        ref[pl.ds(base, 2 * plane), :] = part[: 2 * plane]
        row = 2 * plane
        for f in range(2, 6):
            ref[pl.ds(base + f * plane + side, inner), :] = part[row : row + inner]
            row += inner
        for end, x in ((0, 0), (1, last)):
            for f, y in ((2, 0), (3, last)):
                ref[pl.ds(base + f * plane + x * side, side), :] = ref[
                    pl.ds(base + end * plane + y * side, side), :
                ]
            for f, z in ((4, 0), (5, last)):
                ref[pl.ds(base + f * plane + x * side, side), :] = ref[
                    pl.ds(base + end * plane + z, side, stride=side), :
                ]


def cut_surface(wide, faces, slot, side):
    plane = side * side
    last = side - 1
    base = slot * 6 * plane
    for p in range(wide.shape[0]):
        for n, x in enumerate((0, last)):
            faces[p, pl.ds(base + n * plane, plane), :] = wide[
                p, pl.ds(x * plane, plane), :
            ]
        for n, y in ((2, 0), (3, last)):
            for x in range(side):
                faces[p, pl.ds(base + n * plane + x * side, side), :] = wide[
                    p, pl.ds(x * plane + y * side, side), :
                ]
        for n, z in ((4, 0), (5, last)):
            faces[p, pl.ds(base + n * plane, plane), :] = wide.at[p][
                pl.ds(z, plane, stride=side), :
            ]


def pack_kernel(x_ref, out_ref, *refs, side):
    *pieces_out, wide = refs
    fill(wide, 0, x_ref[...].astype(F32))
    pack_surface(wide, out_ref, side, x_ref.shape[1])
    share(x_ref[...], pieces_out)


def share(value, refs):
    for n, ref in enumerate(refs):
        count = ref.shape[0]
        ref[...] = value[n * count : (n + 1) * count]


def weight_rows(width, tap):
    return [
        (lane, 9 * lane + tap * lanes, lanes) for _, lane, lanes in pieces(width)
    ]


def weights_kernel(own_ref, other_ref, out_ref):
    core = lax.axis_index("wt")
    taps, depth, both = own_ref.shape
    width = out_ref.shape[2]
    half = depth * (both // width)
    step = 16
    for tap in range(taps):
        rows = {}
        for channel, row, count in weight_rows(width, tap % 9):
            for n in range(0, count, step):
                rows[channel + n] = row + n
        for ref, place in ((own_ref, core), (other_ref, 1 - core)):
            for group in range(both // width):
                lane = group * width
                value = ref[tap, :, lane : lane + width]
                for n in range(0, depth, step):
                    at = group * depth + n
                    row = jnp.where(place == 0, rows[at], rows[at + half])
                    row = pl.multiple_of(row, step)
                    out_ref[tap // 9, pl.ds(row, step), :] = value[n : n + step]


def tap_weights(w, tap):
    third, tap = divmod(tap, 9)
    return jnp.concatenate(
        [w[third, pl.ds(row, count), :] for _, row, count in weight_rows(w.shape[2], tap)],
        axis=0,
    )


def shifts(middle, low, high, mask):
    side = middle.shape[1]
    return (
        pltpu.roll(jnp.where(mask == side - 1, low, middle), 1, axis=1),
        middle,
        pltpu.roll(jnp.where(mask == 0, high, middle), side - 1, axis=1),
    )


def inside_kernel(*refs, side, block_of):
    table_ref, beside, *centers, w, total, near, masks = refs[:-5]
    wide, faces, lhs, table, semaphore = refs[-5:]
    copy = pltpu.make_async_copy(table_ref, table, semaphore)
    copy.start()
    width = w.shape[2]
    plane = side * side
    for n, part in enumerate(centers):
        fill(wide, n * part.shape[0], part[...].astype(F32))
    mask = lax.broadcasted_iota(jnp.int32, (side, side, LANES), 1)
    nothing = jnp.zeros((side, side, LANES), F32)
    edge = jnp.zeros((1, side, LANES), F32)
    for p, lane, lanes in pieces(width):
        folds = LANES // lanes
        for x in range(side):
            middle = wide[p, pl.ds(x * plane, plane), :].reshape(side, side, LANES)
            if folds > 1:
                position = lax.broadcasted_iota(jnp.int32, middle.shape, 2)
                for n in range(1, folds):
                    turned = pltpu.roll(middle, n * lanes, axis=2)
                    middle = jnp.where(position >= n * lanes, turned, middle)
            moved = shifts(middle, nothing, nothing, mask)
            taps = []
            for j in range(3):
                for k in range(3):
                    value = moved[k]
                    if j == 0:
                        value = jnp.concatenate([edge, value[: side - 1]], axis=0)
                    elif j == 2:
                        value = jnp.concatenate([value[1:], edge], axis=0)
                    taps.append(value.reshape(plane, LANES))
            for t in range(0, 9, folds):
                value = taps[t]
                used = min(folds, 9 - t)
                for n in range(1, used):
                    position = lax.broadcasted_iota(jnp.int32, value.shape, 1)
                    value = jnp.where(position >= n * lanes, taps[t + n], value)
                at = 9 * lane + t * lanes
                lhs[pl.ds(x * plane, plane), at : at + used * lanes] = value[
                    :, : used * lanes
                ].astype(BF16)
    for i in (1, 0, 2):
        first, source, count = (1, 0, 0)[i], (0, 0, 1)[i], side - (i != 1)
        acc = jnp.dot(
            lhs[pl.ds(source * plane, count * plane), :],
            w[i],
            preferred_element_type=F32,
        )
        for p, lane, lanes in pieces(width):
            part = acc[:, lane : lane + lanes]
            place = pl.ds(first * plane, count * plane)
            if i == 1:
                total[p, place, 0:lanes] = part
            else:
                total[p, place, 0:lanes] += part
    fill(faces, 0, jnp.zeros((6 * plane, width), F32))
    spread_surface(beside, faces, 1, side, width)
    cut_surface(wide, faces, 2, side)
    copy.wait()
    choose_near(table, block_of(), faces, near, masks, side)


def borders(side):
    last = side - 1
    for group in range(6):
        axis, up = divmod(group, 2)
        face = 2 * axis + 1 - up
        sign = 2 * up - 1
        for to, count, row, b in (
            (0, 1, last * side, -1),
            (1, side, 0, 0),
            (side + 1, 1, 0, 1),
        ):
            offsets = {}
            for c in (-1, 0, 1):
                if axis == 0:
                    offsets[c] = (sign, b, c)
                elif axis == 1 and b == 0:
                    offsets[c] = (0, sign, c)
                elif axis == 2 and b == 0 and c == 0:
                    offsets[c] = (0, 0, sign)
            yield group, to, count, row, face, offsets


def entry(offset):
    a, b, c = offset
    return 9 * (a + 1) + 3 * (b + 1) + c + 1


def choose_near(table, block, faces, near, masks, side):
    plane = side * side
    pair = block + 1 - 2 * lax.rem(block, 2)

    def slot(n):
        return jnp.where(n < 0, 0, jnp.where(n == block, 2, jnp.where(n == pair, 1, 3)))

    slots = [slot(table[0, t]) for t in range(27)]
    for t, value in enumerate(slots):
        flag = (value > 0 if t == 13 else value == 3).astype(F32)
        masks[pl.ds(8 * t, 8), :] = jnp.full((8, LANES), flag, F32)
    for group, to, count, row, face, offsets in borders(side):
        for c, offset in offsets.items():
            value = slots[entry(offset)]
            source = jnp.where(value == 3, 0, value)
            start = pl.multiple_of((source * 6 + face) * plane + row, side)
            place = pl.ds(((3 * group + c + 1) * (side + 2) + to) * side, count * side)
            for p in range(faces.shape[0]):
                near[p, place, :] = faces[p, pl.ds(start, count * side), :]


def add_outside(far, w, near, masks, total, faces, even, odd, side):
    width = w.shape[2]
    plane = side * side
    last = side - 1
    spread_surface(far, faces, 0, side, width)
    mask = lax.broadcasted_iota(jnp.int32, (side, side, LANES), 1)
    for group, to, count, row, face, offsets in borders(side):
        for p, lane, lanes in pieces(width):
            place = pl.ds(to * side, count * side)
            if not offsets:
                blank = jnp.zeros((3, side, lanes), BF16)
                even[group, :, place, lane : lane + lanes] = blank
                continue

            def chunk(c):
                if c not in offsets:
                    return jnp.zeros((count, side, LANES), F32)
                away = masks[pl.ds(8 * entry(offsets[c]), 8), :] > 0
                at = ((3 * group + c + 1) * (side + 2) + to) * side
                afar = faces[p, pl.ds(face * plane + row, count * side), :]
                here = near[p, pl.ds(at, count * side), :]
                shape = (count, side, LANES)
                return jnp.where(
                    jnp.broadcast_to(away[None], shape),
                    afar.reshape(shape),
                    here.reshape(shape),
                )

            moved = shifts(chunk(0), chunk(-1), chunk(1), mask[:count])
            for k, value in enumerate(moved):
                value = value.reshape(count * side, LANES)[:, :lanes]
                if count == side:
                    odd[group, k, :, lane : lane + lanes] = value.astype(BF16)
                even[group, k, place, lane : lane + lanes] = value.astype(BF16)

    sums = [None] * 6
    for i in range(3):
        for j in range(3):
            for k in range(3):
                parts, groups = [], []
                for axis, tap, chunk, shift in ((0, i, j, k), (1, j, i, k), (2, k, i, j)):
                    if tap == 1:
                        continue
                    group = 2 * axis + tap // 2
                    if chunk == 1:
                        parts.append(odd[group, shift])
                    else:
                        parts.append(
                            even[group, shift, chunk * side : chunk * side + plane]
                        )
                    groups.append(group)
                if not parts:
                    continue
                product = jnp.dot(
                    jnp.concatenate(parts, axis=0),
                    tap_weights(w, 9 * i + 3 * j + k),
                    preferred_element_type=F32,
                )
                for n, group in enumerate(groups):
                    part = product[n * plane : (n + 1) * plane]
                    sums[group] = part if sums[group] is None else sums[group] + part

    for p, lane, lanes in pieces(width):
        ref = total.at[p]
        part = [value[:, lane : lane + lanes] for value in sums]
        if lanes < LANES:
            pad = jnp.zeros((plane, LANES - lanes), F32)
            part = [jnp.concatenate([value, pad], axis=1) for value in part]
        for up, x in ((0, 0), (1, last)):
            ref[pl.ds(x * plane, plane), :] += part[up]
        for up, y in ((0, 0), (1, last)):
            for x in range(side):
                ref[pl.ds(x * plane + y * side, side), :] += part[2 + up][
                    x * side : (x + 1) * side
                ]
        for up, z in ((0, 0), (1, last)):
            ref[pl.ds(z, plane, stride=side), :] += part[4 + up]


def first_kernel(far, w, total_in, near, masks, surface, *refs, side):
    *outs, total, faces, even, odd = refs
    add_outside(far, w, near, masks, total, faces, even, odd, side)
    active = masks[pl.ds(8 * 13, 1), :]

    def change(value):
        return jnp.maximum(value, 0.0) * active[:, : value.shape[1]]

    pack_surface(total, surface, side, w.shape[2], change)
    for p, lane, lanes in pieces(w.shape[2]):
        for n, out in enumerate(outs):
            count = out.shape[0]
            value = change(total[p, pl.ds(n * count, count), 0:lanes])
            out[:, lane : lane + lanes] = value.astype(BF16)


def second_kernel(
    occupancy, far, w, features, total_in, near, masks, out, total, faces, even, odd, *, side
):
    add_outside(far, w, near, masks, total, faces, even, odd, side)
    active = occupancy[...].astype(F32)
    for p, lane, lanes in pieces(w.shape[2]):
        value = features[:, lane : lane + lanes].astype(F32) + total[p, :, 0:lanes]
        out[:, lane : lane + lanes] = jnp.maximum(value, 0.0) * active


def first_block():
    return 2 * lax.axis_index("space") + 1 - lax.axis_index("wt")


def second_block():
    return 2 * lax.axis_index("space") + lax.axis_index("wt")


def call(kernel, operands, outs, scratch=(), anywhere=0, cost=0, aliases={}):
    outs = [jax.ShapeDtypeStruct(shape, kind) for shape, kind in outs]
    result = pl.pallas_call(
        kernel,
        out_shape=outs,
        in_specs=[pl.BlockSpec(memory_space=pl.ANY)] * anywhere
        + [pl.BlockSpec(memory_space=VMEM)] * (len(operands) - anywhere),
        out_specs=[pl.BlockSpec(memory_space=VMEM)] * len(outs),
        scratch_shapes=list(scratch),
        input_output_aliases=aliases,
        compiler_params=pltpu.CompilerParams(vmem_limit_bytes=32 * 2**20),
        cost_estimate=pl.CostEstimate(flops=cost, bytes_accessed=0, transcendentals=0),
    )(*operands)
    return result[0] if len(outs) == 1 else result


def body(features, occupancy, neighbours, kernel_one, kernel_two):
    side, width = features.shape[1], features.shape[4]
    rows, plane = side**3, side * side
    total = lax.axis_size(AXES)
    halves = [(i, i ^ 1) for i in range(total)]
    cycle = [(i, i - 2) if i % 2 == 0 else (i, i + 2) for i in range(total)]
    cycle[0], cycle[-1] = (0, 1), (total - 1, total - 2)
    back = [(j, i) for i, j in cycle]
    face = ((folded_rows(side, width), LANES), BF16)
    piece = ((rows // PARTS, width), BF16)
    wide = ((rows, width), F32)
    count = len(pieces(width))

    own = features.reshape(rows, width)
    own_face, *own_parts = call(
        functools.partial(pack_kernel, side=side),
        (own,),
        [face] + [piece] * PARTS,
        [VMEM((count, rows, LANES), F32)],
        cost=PACK_COST,
    )
    table_other = lax.ppermute(neighbours, AXES, halves)
    other = [lax.ppermute(part, AXES, halves) for part in own_parts]
    far = lax.ppermute(own_face, AXES, cycle)

    def weights(kernel):
        flat = kernel.reshape((27,) + kernel.shape[3:])
        swapped = lax.ppermute(flat, AXES, halves)
        return call(weights_kernel, (flat, swapped), [((3, 9 * width, width), BF16)])

    w_one, w_two = weights(kernel_one), weights(kernel_two)

    sums = ((count, rows, LANES), F32)
    near = ((count, 6 * 3 * (side + 2) * side, LANES), F32)
    masks = ((27 * 8, LANES), F32)

    def inside(block_of, table, beside, center, w):
        return call(
            functools.partial(inside_kernel, side=side, block_of=block_of),
            (table, beside, *center, w),
            [sums, near, masks],
            [
                VMEM((count, rows, LANES), F32),
                VMEM((count, 3 * 6 * plane, LANES), F32),
                VMEM((rows, 9 * width), BF16),
                SMEM(table.shape, jnp.int32),
                pltpu.SemaphoreType.DMA,
            ],
            anywhere=1,
        )

    planes = [
        VMEM((count, 6 * plane, LANES), F32),
        VMEM((6, 3, plane + 2 * side, width), BF16),
        VMEM((6, 3, plane, width), BF16),
    ]
    hidden_face, *hidden, _ = call(
        functools.partial(first_kernel, side=side),
        (far, w_one, *inside(first_block, table_other, own_face, other, w_one)),
        [face] + [piece] * PARTS + [sums],
        planes,
        aliases={2: 1 + PARTS},
        cost=FIRST_COST,
    )
    hidden_own = [lax.ppermute(part, AXES, halves) for part in hidden]
    hidden_far = lax.ppermute(hidden_face, AXES, back)
    out, _ = call(
        functools.partial(second_kernel, side=side),
        (
            occupancy.reshape(1, 1),
            hidden_far,
            w_two,
            own,
            *inside(second_block, neighbours, hidden_face, hidden_own, w_two),
        ),
        [wide, sums],
        planes,
        aliases={4: 1},
    )
    return out.reshape((1, side, side, side, width))


def solution(mesh):
    return jax.shard_map(
        body,
        mesh=mesh,
        in_specs=(
            P(AXES, None, None, None, None),
            P(AXES),
            P(AXES, None),
            P(None, None, None, None, "wt"),
            P(None, None, None, None, "wt"),
        ),
        out_specs=P(AXES, None, None, None, None),
        check_vma=False,
    )
```

```python
import functools

import jax
import jax.numpy as jnp
from jax import lax
from jax.experimental import pallas as pl
from jax.experimental.pallas import tpu as pltpu
from jax.sharding import PartitionSpec as P

PARTS = 2
MARK_COST = 65 * 10**7
NEXT_COST = 30 * 10**7
PACK_COST = 4 * 10**9
FIRST_COST = 18 * 10**9
AXES = ("space", "wt")
VMEM = pltpu.VMEM
SMEM = pltpu.SMEM
LANES = 128
F32 = jnp.float32
BF16 = jnp.bfloat16


def pieces(width):
    return [
        (p, p * LANES, min(LANES, width - p * LANES)) for p in range(-(-width // LANES))
    ]


def fill(wide, base, value):
    rows, width = value.shape
    for p, lane, lanes in pieces(width):
        wide[p, pl.ds(base, rows), 0:lanes] = value[:, lane : lane + lanes]


def surface_rows(side):
    return 2 * side * side + 4 * (side - 2) * side


def folded_rows(side, width):
    return -(-surface_rows(side) * width // LANES)


def pack_surface(wide, out_ref, side, width, change=lambda value: value):
    plane = side * side
    inner = (side - 2) * side
    last = side - 1
    rows = surface_rows(side)
    for p, lane, lanes in pieces(width):
        ref = wide.at[p]
        parts = [ref[pl.ds(0, plane), :], ref[pl.ds(last * plane, plane), :]]
        for y in (0, last):
            for x in range(1, last):
                parts.append(ref[pl.ds(x * plane + y * side, side), :])
        for z in (0, last):
            parts.append(ref[pl.ds(plane + z, inner, stride=side), :])
        value = change(jnp.concatenate(parts, axis=0))
        folds = LANES // lanes
        count = rows // folds
        result = value[:count]
        position = lax.broadcasted_iota(jnp.int32, (count, LANES), 1)
        for n in range(1, folds):
            part = pltpu.roll(value[n * count : (n + 1) * count], n * lanes, axis=1)
            result = jnp.where(position >= n * lanes, part, result)
        out_ref[pl.ds(p * rows, count), :] = result.astype(BF16)


def spread_surface(packed_ref, faces, slot, side, width):
    plane = side * side
    inner = (side - 2) * side
    last = side - 1
    base = slot * 6 * plane
    rows = surface_rows(side)
    for p, lane, lanes in pieces(width):
        ref = faces.at[p]
        folds = LANES // lanes
        part = packed_ref[pl.ds(p * rows, rows // folds), :].astype(F32)
        if folds > 1:
            turned = [part] + [
                pltpu.roll(part, LANES - n * lanes, axis=1) for n in range(1, folds)
            ]
            part = jnp.concatenate(turned, axis=0)
        ref[pl.ds(base, 2 * plane), :] = part[: 2 * plane]
        row = 2 * plane
        for f in range(2, 6):
            ref[pl.ds(base + f * plane + side, inner), :] = part[row : row + inner]
            row += inner
        for end, x in ((0, 0), (1, last)):
            for f, y in ((2, 0), (3, last)):
                ref[pl.ds(base + f * plane + x * side, side), :] = ref[
                    pl.ds(base + end * plane + y * side, side), :
                ]
            for f, z in ((4, 0), (5, last)):
                ref[pl.ds(base + f * plane + x * side, side), :] = ref[
                    pl.ds(base + end * plane + z, side, stride=side), :
                ]


def cut_surface(wide, faces, slot, side):
    plane = side * side
    last = side - 1
    base = slot * 6 * plane
    for p in range(wide.shape[0]):
        for n, x in enumerate((0, last)):
            faces[p, pl.ds(base + n * plane, plane), :] = wide[
                p, pl.ds(x * plane, plane), :
            ]
        for n, y in ((2, 0), (3, last)):
            for x in range(side):
                faces[p, pl.ds(base + n * plane + x * side, side), :] = wide[
                    p, pl.ds(x * plane + y * side, side), :
                ]
        for n, z in ((4, 0), (5, last)):
            faces[p, pl.ds(base + n * plane, plane), :] = wide.at[p][
                pl.ds(z, plane, stride=side), :
            ]


def mark_kernel(out_ref):
    out_ref[...] = jnp.zeros(out_ref.shape, out_ref.dtype)


def pack_kernel(x_ref, mark, after, out_ref, *refs, side):
    *pieces_out, wide = refs
    fill(wide, 0, x_ref[...].astype(F32))
    pack_surface(wide, out_ref, side, x_ref.shape[1])
    share(x_ref[...], pieces_out)


def share(value, refs):
    for n, ref in enumerate(refs):
        count = ref.shape[0]
        ref[...] = value[n * count : (n + 1) * count]


def weight_rows(width, tap):
    return [
        (lane, 9 * lane + tap * lanes, lanes) for _, lane, lanes in pieces(width)
    ]


def weights_kernel(own_ref, other_ref, out_ref):
    core = lax.axis_index("wt")
    taps, depth, both = own_ref.shape
    width = out_ref.shape[2]
    half = depth * (both // width)
    step = 16
    for tap in range(taps):
        rows = {}
        for channel, row, count in weight_rows(width, tap % 9):
            for n in range(0, count, step):
                rows[channel + n] = row + n
        for ref, place in ((own_ref, core), (other_ref, 1 - core)):
            for group in range(both // width):
                lane = group * width
                value = ref[tap, :, lane : lane + width]
                for n in range(0, depth, step):
                    at = group * depth + n
                    row = jnp.where(place == 0, rows[at], rows[at + half])
                    row = pl.multiple_of(row, step)
                    out_ref[tap // 9, pl.ds(row, step), :] = value[n : n + step]


def tap_weights(w, tap):
    third, tap = divmod(tap, 9)
    return jnp.concatenate(
        [w[third, pl.ds(row, count), :] for _, row, count in weight_rows(w.shape[2], tap)],
        axis=0,
    )


def shifts(middle, low, high, mask):
    side = middle.shape[1]
    return (
        pltpu.roll(jnp.where(mask == side - 1, low, middle), 1, axis=1),
        middle,
        pltpu.roll(jnp.where(mask == 0, high, middle), side - 1, axis=1),
    )


def turned_chip(chips):
    chip = lax.axis_index("space")
    return ((chip == 0) | (chip == chips - 1)).astype(jnp.int32)


def inside_kernel(*refs, side, chips, counts, opening):
    refs = list(refs)
    table_refs, *sources = [[refs.pop(0) for _ in range(n)] for n in counts]
    w, total, near, masks, wide, faces, lhs, tables, semaphores = refs
    copies = [
        pltpu.make_async_copy(ref, tables.at[n], semaphores.at[n])
        for n, ref in enumerate(table_refs)
    ]
    for copy in copies:
        copy.start()
    width = w.shape[2]
    plane = side * side
    turned = turned_chip(chips)
    home = 2 * lax.axis_index("space") + lax.axis_index("wt")
    other = home + 1 - 2 * lax.axis_index("wt")
    away = jnp.where(turned == 1, other, home)
    ids = (home, other) if opening else (away, home + other - away)
    for slot, parts in enumerate(sources):
        for n, part in enumerate(parts):
            fill(wide.at[slot], n * part.shape[0], part[...].astype(F32))
    mask = lax.broadcasted_iota(jnp.int32, (side, side, LANES), 1)
    nothing = jnp.zeros((side, side, LANES), F32)
    edge = jnp.zeros((1, side, LANES), F32)
    for p, lane, lanes in pieces(width):
        folds = LANES // lanes
        for x in range(side):
            middle = wide[turned, p, pl.ds(x * plane, plane), :]
            middle = middle.reshape(side, side, LANES)
            if folds > 1:
                position = lax.broadcasted_iota(jnp.int32, middle.shape, 2)
                for n in range(1, folds):
                    moved = pltpu.roll(middle, n * lanes, axis=2)
                    middle = jnp.where(position >= n * lanes, moved, middle)
            moved = shifts(middle, nothing, nothing, mask)
            taps = []
            for j in range(3):
                for k in range(3):
                    value = moved[k]
                    if j == 0:
                        value = jnp.concatenate([edge, value[: side - 1]], axis=0)
                    elif j == 2:
                        value = jnp.concatenate([value[1:], edge], axis=0)
                    taps.append(value.reshape(plane, LANES))
            for t in range(0, 9, folds):
                value = taps[t]
                used = min(folds, 9 - t)
                for n in range(1, used):
                    position = lax.broadcasted_iota(jnp.int32, value.shape, 1)
                    value = jnp.where(position >= n * lanes, taps[t + n], value)
                at = 9 * lane + t * lanes
                lhs[pl.ds(x * plane, plane), at : at + used * lanes] = value[
                    :, : used * lanes
                ].astype(BF16)
    for i in (1, 0, 2):
        first, source, count = (1, 0, 0)[i], (0, 0, 1)[i], side - (i != 1)
        acc = jnp.dot(
            lhs[pl.ds(source * plane, count * plane), :],
            w[i],
            preferred_element_type=F32,
        )
        for p, lane, lanes in pieces(width):
            part = acc[:, lane : lane + lanes]
            place = pl.ds(first * plane, count * plane)
            if i == 1:
                total[p, place, 0:lanes] = part
            else:
                total[p, place, 0:lanes] += part
    fill(faces, 0, jnp.zeros((6 * plane, width), F32))
    for slot in range(2):
        cut_surface(wide.at[slot], faces, slot + 1, side)
    for copy in copies:
        copy.wait()
    row = turned if opening else 0
    entries = [tables[row, 0, t] for t in range(27)]
    choose_near(entries, ids, faces, near, masks, side)


def borders(side):
    last = side - 1
    for group in range(6):
        axis, up = divmod(group, 2)
        face = 2 * axis + 1 - up
        sign = 2 * up - 1
        for to, count, row, b in (
            (0, 1, last * side, -1),
            (1, side, 0, 0),
            (side + 1, 1, 0, 1),
        ):
            offsets = {}
            for c in (-1, 0, 1):
                if axis == 0:
                    offsets[c] = (sign, b, c)
                elif axis == 1 and b == 0:
                    offsets[c] = (0, sign, c)
                elif axis == 2 and b == 0 and c == 0:
                    offsets[c] = (0, 0, sign)
            yield group, to, count, row, face, offsets


def entry(offset):
    a, b, c = offset
    return 9 * (a + 1) + 3 * (b + 1) + c + 1


def choose_near(entries, ids, faces, near, masks, side):
    plane = side * side

    def slot(n):
        here = jnp.where(n == ids[0], 1, jnp.where(n == ids[1], 2, 3))
        return jnp.where(n < 0, 0, here)

    slots = [slot(n) for n in entries]
    for t, value in enumerate(slots):
        flag = (value > 0 if t == 13 else value == 3).astype(F32)
        masks[pl.ds(8 * t, 8), :] = jnp.full((8, LANES), flag, F32)
    for group, to, count, row, face, offsets in borders(side):
        for c, offset in offsets.items():
            value = slots[entry(offset)]
            source = jnp.where(value == 3, 0, value)
            start = pl.multiple_of((source * 6 + face) * plane + row, side)
            place = pl.ds(((3 * group + c + 1) * (side + 2) + to) * side, count * side)
            for p in range(faces.shape[0]):
                near[p, place, :] = faces[p, pl.ds(start, count * side), :]


def add_outside(far, w, near, masks, total, faces, even, odd, side):
    width = w.shape[2]
    plane = side * side
    last = side - 1
    spread_surface(far, faces, 0, side, width)
    mask = lax.broadcasted_iota(jnp.int32, (side, side, LANES), 1)
    for group, to, count, row, face, offsets in borders(side):
        for p, lane, lanes in pieces(width):
            place = pl.ds(to * side, count * side)
            if not offsets:
                blank = jnp.zeros((3, side, lanes), BF16)
                even[group, :, place, lane : lane + lanes] = blank
                continue

            def chunk(c):
                if c not in offsets:
                    return jnp.zeros((count, side, LANES), F32)
                away = masks[pl.ds(8 * entry(offsets[c]), 8), :] > 0
                at = ((3 * group + c + 1) * (side + 2) + to) * side
                afar = faces[p, pl.ds(face * plane + row, count * side), :]
                here = near[p, pl.ds(at, count * side), :]
                shape = (count, side, LANES)
                return jnp.where(
                    jnp.broadcast_to(away[None], shape),
                    afar.reshape(shape),
                    here.reshape(shape),
                )

            moved = shifts(chunk(0), chunk(-1), chunk(1), mask[:count])
            for k, value in enumerate(moved):
                value = value.reshape(count * side, LANES)[:, :lanes]
                if count == side:
                    odd[group, k, :, lane : lane + lanes] = value.astype(BF16)
                even[group, k, place, lane : lane + lanes] = value.astype(BF16)

    sums = [None] * 6
    for i in range(3):
        for j in range(3):
            for k in range(3):
                parts, groups = [], []
                for axis, tap, chunk, shift in ((0, i, j, k), (1, j, i, k), (2, k, i, j)):
                    if tap == 1:
                        continue
                    group = 2 * axis + tap // 2
                    if chunk == 1:
                        parts.append(odd[group, shift])
                    else:
                        parts.append(
                            even[group, shift, chunk * side : chunk * side + plane]
                        )
                    groups.append(group)
                if not parts:
                    continue
                product = jnp.dot(
                    jnp.concatenate(parts, axis=0),
                    tap_weights(w, 9 * i + 3 * j + k),
                    preferred_element_type=F32,
                )
                for n, group in enumerate(groups):
                    part = product[n * plane : (n + 1) * plane]
                    sums[group] = part if sums[group] is None else sums[group] + part

    for p, lane, lanes in pieces(width):
        ref = total.at[p]
        part = [value[:, lane : lane + lanes] for value in sums]
        if lanes < LANES:
            pad = jnp.zeros((plane, LANES - lanes), F32)
            part = [jnp.concatenate([value, pad], axis=1) for value in part]
        for up, x in ((0, 0), (1, last)):
            ref[pl.ds(x * plane, plane), :] += part[up]
        for up, y in ((0, 0), (1, last)):
            for x in range(side):
                ref[pl.ds(x * plane + y * side, side), :] += part[2 + up][
                    x * side : (x + 1) * side
                ]
        for up, z in ((0, 0), (1, last)):
            ref[pl.ds(z, plane, stride=side), :] += part[4 + up]


def first_kernel(far, w, total_in, near, masks, surface, *refs, side):
    *outs, total, faces, even, odd = refs
    add_outside(far, w, near, masks, total, faces, even, odd, side)
    active = masks[pl.ds(8 * 13, 1), :]

    def change(value):
        return jnp.maximum(value, 0.0) * active[:, : value.shape[1]]

    pack_surface(total, surface, side, w.shape[2], change)
    for p, lane, lanes in pieces(w.shape[2]):
        for n, out in enumerate(outs):
            count = out.shape[0]
            value = change(total[p, pl.ds(n * count, count), 0:lanes])
            out[:, lane : lane + lanes] = value.astype(BF16)


def second_kernel(
    occupancy, far, w, features, total_in, near, masks, out, total, faces, even, odd, *, side
):
    add_outside(far, w, near, masks, total, faces, even, odd, side)
    active = occupancy[...].astype(F32)
    for p, lane, lanes in pieces(w.shape[2]):
        value = features[:, lane : lane + lanes].astype(F32) + total[p, :, 0:lanes]
        out[:, lane : lane + lanes] = jnp.maximum(value, 0.0) * active


def chip_exchanges(chips):
    def end(chip):
        return int(chip in (0, chips - 1))

    last = 2 * chips - 1
    first, second = [(0, 1), (last, last - 1)], [(1, 0), (last - 1, last)]
    for c in range(chips - 1):
        up, down = 2 * c, 2 * (c + 1)
        first.append((up + 1, down + end(c + 1)))
        first.append((down, up + 1 - end(c)))
        second.append((up + 1 - end(c), down))
        second.append((down + end(c + 1), up + 1))
    return first, second


def call(kernel, operands, outs, scratch=(), anywhere=0, cost=0, aliases={}):
    outs = [jax.ShapeDtypeStruct(shape, kind) for shape, kind in outs]
    result = pl.pallas_call(
        kernel,
        out_shape=outs,
        in_specs=[pl.BlockSpec(memory_space=pl.ANY)] * anywhere
        + [pl.BlockSpec(memory_space=VMEM)] * (len(operands) - anywhere),
        out_specs=[pl.BlockSpec(memory_space=VMEM)] * len(outs),
        scratch_shapes=list(scratch),
        input_output_aliases=aliases,
        compiler_params=pltpu.CompilerParams(vmem_limit_bytes=32 * 2**20),
        cost_estimate=pl.CostEstimate(flops=cost, bytes_accessed=0, transcendentals=0),
    )(*operands)
    return result[0] if len(outs) == 1 else result


def body(features, occupancy, neighbours, kernel_one, kernel_two):
    side, width = features.shape[1], features.shape[4]
    rows, plane = side**3, side * side
    total = lax.axis_size(AXES)
    halves = [(i, i ^ 1) for i in range(total)]
    chips = total // 2
    first, second = chip_exchanges(chips)
    face = ((folded_rows(side, width), LANES), BF16)
    piece = ((rows // PARTS, width), BF16)
    wide = ((rows, width), F32)
    count = len(pieces(width))

    own = features.reshape(rows, width)
    mark = call(mark_kernel, (), [((8, LANES), F32)], cost=MARK_COST)
    mark, one_late = lax.optimization_barrier((mark, kernel_one))
    after = call(mark_kernel, (), [((8, LANES), F32)], cost=NEXT_COST)
    own_face, *own_parts = call(
        functools.partial(pack_kernel, side=side),
        (own, mark, after),
        [face] + [piece] * PARTS,
        [VMEM((count, rows, LANES), F32)],
        cost=PACK_COST,
    )
    table_other = lax.ppermute(neighbours, AXES, halves)
    other = [lax.ppermute(part, AXES, halves) for part in own_parts]
    far = lax.ppermute(own_face, AXES, first)

    def weights(kernel, late):
        flat = kernel.reshape((27,) + kernel.shape[3:])
        swapped = lax.ppermute(late.reshape(flat.shape), AXES, halves)
        return call(weights_kernel, (flat, swapped), [((3, 9 * width, width), BF16)])

    w_one, w_two = weights(kernel_one, one_late), weights(kernel_two, kernel_two)

    sums = ((count, rows, LANES), F32)
    near = ((count, 6 * 3 * (side + 2) * side, LANES), F32)
    masks = ((27 * 8, LANES), F32)

    def inside(layer, tables, here, there, w):
        counts = (len(tables), len(here), len(there))
        return call(
            functools.partial(
                inside_kernel, side=side, chips=chips, counts=counts, opening=layer == 0
            ),
            (*tables, *here, *there, w),
            [sums, near, masks],
            [
                VMEM((2, count, rows, LANES), F32),
                VMEM((count, 3 * 6 * plane, LANES), F32),
                VMEM((rows, 9 * width), BF16),
                SMEM((len(tables),) + neighbours.shape, jnp.int32),
                pltpu.SemaphoreType.DMA((len(tables),)),
            ],
            anywhere=len(tables),
        )

    planes = [
        VMEM((count, 6 * plane, LANES), F32),
        VMEM((6, 3, plane + 2 * side, width), BF16),
        VMEM((6, 3, plane, width), BF16),
    ]
    hidden_face, *hidden, _ = call(
        functools.partial(first_kernel, side=side),
        (far, w_one, *inside(0, (neighbours, table_other), own_parts, other, w_one)),
        [face] + [piece] * PARTS + [sums],
        planes,
        aliases={2: 1 + PARTS},
        cost=FIRST_COST,
    )
    hidden_other = [lax.ppermute(part, AXES, halves) for part in hidden]
    hidden_far = lax.ppermute(hidden_face, AXES, second)
    out, _ = call(
        functools.partial(second_kernel, side=side),
        (
            occupancy.reshape(1, 1),
            hidden_far,
            w_two,
            own,
            *inside(1, (neighbours,), hidden, hidden_other, w_two),
        ),
        [wide, sums],
        planes,
        aliases={4: 1},
    )
    return out.reshape((1, side, side, side, width))


def solution(mesh):
    return jax.shard_map(
        body,
        mesh=mesh,
        in_specs=(
            P(AXES, None, None, None, None),
            P(AXES),
            P(AXES, None),
            P(None, None, None, None, "wt"),
            P(None, None, None, None, "wt"),
        ),
        out_specs=P(AXES, None, None, None, None),
        check_vma=False,
    )
```

```python
import functools

import jax
import jax.numpy as jnp
from jax import lax
from jax.experimental import pallas as pl
from jax.experimental.pallas import tpu as pltpu
from jax.sharding import PartitionSpec as P

PARTS = 2
MARK_COST = 65 * 10**7
NEXT_COST = 30 * 10**7
PACK_COST = 4 * 10**9
FIRST_COST = 18 * 10**9
AXES = ("space", "wt")
VMEM = pltpu.VMEM
SMEM = pltpu.SMEM
LANES = 128
F32 = jnp.float32
BF16 = jnp.bfloat16


def pieces(width):
    return [
        (p, p * LANES, min(LANES, width - p * LANES)) for p in range(-(-width // LANES))
    ]


def fill(wide, base, value):
    rows, width = value.shape
    for p, lane, lanes in pieces(width):
        wide[p, pl.ds(base, rows), 0:lanes] = value[:, lane : lane + lanes]


def surface_rows(side):
    return side**3 - (side - 2) ** 3


def folded_shape(side, lanes):
    rows, folds = surface_rows(side), LANES // lanes
    short = rows // folds // 16 * 16
    return folds, short, rows - folds * short


def folded_rows(side, width):
    rows = 0
    for p, lane, lanes in pieces(width):
        folds, short, left = folded_shape(side, lanes)
        rows += surface_rows(side) if folds == 1 else short + left
    return -(-rows // 16) * 16


def folded_start(side, width):
    rows = surface_rows(side) * (width // LANES)
    for p, lane, lanes in pieces(width):
        if lanes < LANES:
            rows += folded_shape(side, lanes)[2]
    return -(-rows // 16) * 16


def pack_surface(wide, out_ref, side, width, change=lambda value: value):
    plane = side * side
    last = side - 1
    rows = surface_rows(side)
    start = folded_start(side, width)
    whole = []
    for p, lane, lanes in pieces(width):
        ref = wide.at[p]
        parts = [ref[pl.ds(0, plane), :], ref[pl.ds(last * plane, plane), :]]
        for y in (0, last):
            for x in range(1, last):
                parts.append(ref[pl.ds(x * plane + y * side, side), :])
        for z in (0, last):
            for x in range(1, last):
                at = x * plane + side + z
                parts.append(ref[pl.ds(at, side - 2, stride=side), :])
        value = change(jnp.concatenate(parts, axis=0))
        folds, count, left = folded_shape(side, lanes)
        if folds == 1:
            whole.append(value)
            continue
        whole.append(value[folds * count :])
        result = value[:count]
        position = lax.broadcasted_iota(jnp.int32, (count, LANES), 1)
        for n in range(1, folds):
            part = pltpu.roll(value[n * count : (n + 1) * count], n * lanes, axis=1)
            result = jnp.where(position >= n * lanes, part, result)
        out_ref[pl.ds(start, count), :] = result.astype(BF16)
    value = jnp.concatenate(whole, axis=0)
    if value.shape[0] < start:
        rest = jnp.zeros((start - value.shape[0], LANES), F32)
        value = jnp.concatenate([value, rest], axis=0)
    out_ref[pl.ds(0, start), :] = value.astype(BF16)


def spread_surface(packed_ref, faces, slot, side, width):
    plane = side * side
    inner = (side - 2) * side
    last = side - 1
    base = slot * 6 * plane
    rows = surface_rows(side)
    start = folded_start(side, width)
    whole = packed_ref[pl.ds(0, start), :].astype(F32)
    for p, lane, lanes in pieces(width):
        ref = faces.at[p]
        folds, count, left = folded_shape(side, lanes)
        if folds == 1:
            part = whole[p * rows : (p + 1) * rows]
        else:
            part = packed_ref[pl.ds(start, count), :].astype(F32)
            turned = [part] + [
                pltpu.roll(part, LANES - n * lanes, axis=1) for n in range(1, folds)
            ]
            turned.append(whole[p * rows : p * rows + left])
            part = jnp.concatenate(turned, axis=0)
        ref[pl.ds(base, 2 * plane), :] = part[: 2 * plane]
        row = 2 * plane
        for f in (2, 3):
            ref[pl.ds(base + f * plane + side, inner), :] = part[row : row + inner]
            row += inner
        for f in (4, 5):
            for x in range(1, last):
                at = base + f * plane + x * side + 1
                ref[pl.ds(at, side - 2), :] = part[row : row + side - 2]
                row += side - 2
        for end, x in ((0, 0), (1, last)):
            for f, y in ((2, 0), (3, last)):
                ref[pl.ds(base + f * plane + x * side, side), :] = ref[
                    pl.ds(base + end * plane + y * side, side), :
                ]
            for f, z in ((4, 0), (5, last)):
                ref[pl.ds(base + f * plane + x * side, side), :] = ref[
                    pl.ds(base + end * plane + z, side, stride=side), :
                ]
        for f, z in ((4, 0), (5, last)):
            for g, y in ((2, 0), (3, last)):
                ref[pl.ds(base + f * plane + y, side, stride=side), :] = ref[
                    pl.ds(base + g * plane + z, side, stride=side), :
                ]


def cut_surface(wide, faces, slot, side):
    plane = side * side
    last = side - 1
    base = slot * 6 * plane
    for p in range(wide.shape[0]):
        for n, x in enumerate((0, last)):
            faces[p, pl.ds(base + n * plane, plane), :] = wide[
                p, pl.ds(x * plane, plane), :
            ]
        for n, y in ((2, 0), (3, last)):
            for x in range(side):
                faces[p, pl.ds(base + n * plane + x * side, side), :] = wide[
                    p, pl.ds(x * plane + y * side, side), :
                ]
        for n, z in ((4, 0), (5, last)):
            faces[p, pl.ds(base + n * plane, plane), :] = wide.at[p][
                pl.ds(z, plane, stride=side), :
            ]


def mark_kernel(out_ref):
    out_ref[...] = jnp.zeros(out_ref.shape, out_ref.dtype)


def pack_kernel(x_ref, mark, after, out_ref, *refs, side):
    *pieces_out, wide = refs
    fill(wide, 0, x_ref[...].astype(F32))
    pack_surface(wide, out_ref, side, x_ref.shape[1])
    share(x_ref[...], pieces_out)


def share(value, refs):
    for n, ref in enumerate(refs):
        count = ref.shape[0]
        ref[...] = value[n * count : (n + 1) * count]


def weight_rows(width, tap):
    return [
        (lane, 9 * lane + tap * lanes, lanes) for _, lane, lanes in pieces(width)
    ]


def weights_kernel(own_ref, other_ref, out_ref):
    core = lax.axis_index("wt")
    taps, depth, both = own_ref.shape
    width = out_ref.shape[2]
    half = depth * (both // width)
    step = 16
    for tap in range(taps):
        rows = {}
        for channel, row, count in weight_rows(width, tap % 9):
            for n in range(0, count, step):
                rows[channel + n] = row + n
        for ref, place in ((own_ref, core), (other_ref, 1 - core)):
            for group in range(both // width):
                lane = group * width
                value = ref[tap, :, lane : lane + width]
                for n in range(0, depth, step):
                    at = group * depth + n
                    row = jnp.where(place == 0, rows[at], rows[at + half])
                    row = pl.multiple_of(row, step)
                    out_ref[tap // 9, pl.ds(row, step), :] = value[n : n + step]


def tap_weights(w, tap):
    third, tap = divmod(tap, 9)
    return jnp.concatenate(
        [w[third, pl.ds(row, count), :] for _, row, count in weight_rows(w.shape[2], tap)],
        axis=0,
    )


def shifts(middle, low, high, mask):
    side = middle.shape[1]
    return (
        pltpu.roll(jnp.where(mask == side - 1, low, middle), 1, axis=1),
        middle,
        pltpu.roll(jnp.where(mask == 0, high, middle), side - 1, axis=1),
    )


def turned_chip(chips):
    chip = lax.axis_index("space")
    return ((chip == 0) | (chip == chips - 1)).astype(jnp.int32)


def inside_kernel(*refs, side, chips, counts, opening):
    refs = list(refs)
    table_refs, *sources = [[refs.pop(0) for _ in range(n)] for n in counts]
    w, total, near, masks, wide, faces, lhs, tables, semaphores = refs
    copies = [
        pltpu.make_async_copy(ref, tables.at[n], semaphores.at[n])
        for n, ref in enumerate(table_refs)
    ]
    for copy in copies:
        copy.start()
    width = w.shape[2]
    plane = side * side
    turned = turned_chip(chips)
    home = 2 * lax.axis_index("space") + lax.axis_index("wt")
    other = home + 1 - 2 * lax.axis_index("wt")
    away = jnp.where(turned == 1, other, home)
    ids = (home, other) if opening else (away, home + other - away)
    for slot, parts in enumerate(sources):
        for n, part in enumerate(parts):
            fill(wide.at[slot], n * part.shape[0], part[...].astype(F32))
    mask = lax.broadcasted_iota(jnp.int32, (side, side, LANES), 1)
    nothing = jnp.zeros((side, side, LANES), F32)
    edge = jnp.zeros((1, side, LANES), F32)
    for p, lane, lanes in pieces(width):
        folds = LANES // lanes
        for x in range(side):
            middle = wide[turned, p, pl.ds(x * plane, plane), :]
            middle = middle.reshape(side, side, LANES)
            if folds > 1:
                position = lax.broadcasted_iota(jnp.int32, middle.shape, 2)
                for n in range(1, folds):
                    moved = pltpu.roll(middle, n * lanes, axis=2)
                    middle = jnp.where(position >= n * lanes, moved, middle)
            moved = shifts(middle, nothing, nothing, mask)
            taps = []
            for j in range(3):
                for k in range(3):
                    value = moved[k]
                    if j == 0:
                        value = jnp.concatenate([edge, value[: side - 1]], axis=0)
                    elif j == 2:
                        value = jnp.concatenate([value[1:], edge], axis=0)
                    taps.append(value.reshape(plane, LANES))
            for t in range(0, 9, folds):
                value = taps[t]
                used = min(folds, 9 - t)
                for n in range(1, used):
                    position = lax.broadcasted_iota(jnp.int32, value.shape, 1)
                    value = jnp.where(position >= n * lanes, taps[t + n], value)
                at = 9 * lane + t * lanes
                lhs[pl.ds(x * plane, plane), at : at + used * lanes] = value[
                    :, : used * lanes
                ].astype(BF16)
    for i in (1, 0, 2):
        first, source, count = (1, 0, 0)[i], (0, 0, 1)[i], side - (i != 1)
        acc = jnp.dot(
            lhs[pl.ds(source * plane, count * plane), :],
            w[i],
            preferred_element_type=F32,
        )
        for p, lane, lanes in pieces(width):
            part = acc[:, lane : lane + lanes]
            place = pl.ds(first * plane, count * plane)
            if i == 1:
                total[p, place, 0:lanes] = part
            else:
                total[p, place, 0:lanes] += part
    fill(faces, 0, jnp.zeros((6 * plane, width), F32))
    for slot in range(2):
        cut_surface(wide.at[slot], faces, slot + 1, side)
    for copy in copies:
        copy.wait()
    row = turned if opening else 0
    entries = [tables[row, 0, t] for t in range(27)]
    choose_near(entries, ids, faces, near, masks, side)


def borders(side):
    last = side - 1
    for group in range(6):
        axis, up = divmod(group, 2)
        face = 2 * axis + 1 - up
        sign = 2 * up - 1
        for to, count, row, b in (
            (0, 1, last * side, -1),
            (1, side, 0, 0),
            (side + 1, 1, 0, 1),
        ):
            offsets = {}
            for c in (-1, 0, 1):
                if axis == 0:
                    offsets[c] = (sign, b, c)
                elif axis == 1 and b == 0:
                    offsets[c] = (0, sign, c)
                elif axis == 2 and b == 0 and c == 0:
                    offsets[c] = (0, 0, sign)
            yield group, to, count, row, face, offsets


def entry(offset):
    a, b, c = offset
    return 9 * (a + 1) + 3 * (b + 1) + c + 1


def choose_near(entries, ids, faces, near, masks, side):
    plane = side * side

    def slot(n):
        here = jnp.where(n == ids[0], 1, jnp.where(n == ids[1], 2, 3))
        return jnp.where(n < 0, 0, here)

    slots = [slot(n) for n in entries]
    for t, value in enumerate(slots):
        flag = (value > 0 if t == 13 else value == 3).astype(F32)
        masks[pl.ds(8 * t, 8), :] = jnp.full((8, LANES), flag, F32)
    for group, to, count, row, face, offsets in borders(side):
        for c, offset in offsets.items():
            value = slots[entry(offset)]
            source = jnp.where(value == 3, 0, value)
            start = pl.multiple_of((source * 6 + face) * plane + row, side)
            place = pl.ds(((3 * group + c + 1) * (side + 2) + to) * side, count * side)
            for p in range(faces.shape[0]):
                near[p, place, :] = faces[p, pl.ds(start, count * side), :]


def add_outside(far, w, near, masks, total, faces, even, odd, side):
    width = w.shape[2]
    plane = side * side
    last = side - 1
    spread_surface(far, faces, 0, side, width)
    mask = lax.broadcasted_iota(jnp.int32, (side, side, LANES), 1)
    for group, to, count, row, face, offsets in borders(side):
        for p, lane, lanes in pieces(width):
            place = pl.ds(to * side, count * side)
            if not offsets:
                blank = jnp.zeros((3, side, lanes), BF16)
                even[group, :, place, lane : lane + lanes] = blank
                continue

            def chunk(c):
                if c not in offsets:
                    return jnp.zeros((count, side, LANES), F32)
                away = masks[pl.ds(8 * entry(offsets[c]), 8), :] > 0
                at = ((3 * group + c + 1) * (side + 2) + to) * side
                afar = faces[p, pl.ds(face * plane + row, count * side), :]
                here = near[p, pl.ds(at, count * side), :]
                shape = (count, side, LANES)
                return jnp.where(
                    jnp.broadcast_to(away[None], shape),
                    afar.reshape(shape),
                    here.reshape(shape),
                )

            moved = shifts(chunk(0), chunk(-1), chunk(1), mask[:count])
            for k, value in enumerate(moved):
                value = value.reshape(count * side, LANES)[:, :lanes]
                if count == side:
                    odd[group, k, :, lane : lane + lanes] = value.astype(BF16)
                even[group, k, place, lane : lane + lanes] = value.astype(BF16)

    sums = [None] * 6
    for i in range(3):
        for j in range(3):
            for k in range(3):
                parts, groups = [], []
                for axis, tap, chunk, shift in ((0, i, j, k), (1, j, i, k), (2, k, i, j)):
                    if tap == 1:
                        continue
                    group = 2 * axis + tap // 2
                    if chunk == 1:
                        parts.append(odd[group, shift])
                    else:
                        parts.append(
                            even[group, shift, chunk * side : chunk * side + plane]
                        )
                    groups.append(group)
                if not parts:
                    continue
                product = jnp.dot(
                    jnp.concatenate(parts, axis=0),
                    tap_weights(w, 9 * i + 3 * j + k),
                    preferred_element_type=F32,
                )
                for n, group in enumerate(groups):
                    part = product[n * plane : (n + 1) * plane]
                    sums[group] = part if sums[group] is None else sums[group] + part

    for p, lane, lanes in pieces(width):
        ref = total.at[p]
        part = [value[:, lane : lane + lanes] for value in sums]
        if lanes < LANES:
            pad = jnp.zeros((plane, LANES - lanes), F32)
            part = [jnp.concatenate([value, pad], axis=1) for value in part]
        for up, x in ((0, 0), (1, last)):
            ref[pl.ds(x * plane, plane), :] += part[up]
        for up, y in ((0, 0), (1, last)):
            for x in range(side):
                ref[pl.ds(x * plane + y * side, side), :] += part[2 + up][
                    x * side : (x + 1) * side
                ]
        for up, z in ((0, 0), (1, last)):
            ref[pl.ds(z, plane, stride=side), :] += part[4 + up]


def first_kernel(far, w, total_in, near, masks, surface, *refs, side):
    *outs, total, faces, even, odd = refs
    add_outside(far, w, near, masks, total, faces, even, odd, side)
    active = masks[pl.ds(8 * 13, 1), :]

    def change(value):
        return jnp.maximum(value, 0.0) * active[:, : value.shape[1]]

    pack_surface(total, surface, side, w.shape[2], change)
    for p, lane, lanes in pieces(w.shape[2]):
        for n, out in enumerate(outs):
            count = out.shape[0]
            value = change(total[p, pl.ds(n * count, count), 0:lanes])
            out[:, lane : lane + lanes] = value.astype(BF16)


def second_kernel(
    occupancy, far, w, features, total_in, near, masks, out, total, faces, even, odd, *, side
):
    add_outside(far, w, near, masks, total, faces, even, odd, side)
    active = occupancy[...].astype(F32)
    for p, lane, lanes in pieces(w.shape[2]):
        value = features[:, lane : lane + lanes].astype(F32) + total[p, :, 0:lanes]
        out[:, lane : lane + lanes] = jnp.maximum(value, 0.0) * active


def chip_exchanges(chips):
    def end(chip):
        return int(chip in (0, chips - 1))

    last = 2 * chips - 1
    first, second = [(0, 1), (last, last - 1)], [(1, 0), (last - 1, last)]
    for c in range(chips - 1):
        up, down = 2 * c, 2 * (c + 1)
        first.append((up + 1, down + end(c + 1)))
        first.append((down, up + 1 - end(c)))
        second.append((up + 1 - end(c), down))
        second.append((down + end(c + 1), up + 1))
    return first, second


def call(kernel, operands, outs, scratch=(), anywhere=0, cost=0, aliases={}):
    outs = [jax.ShapeDtypeStruct(shape, kind) for shape, kind in outs]
    result = pl.pallas_call(
        kernel,
        out_shape=outs,
        in_specs=[pl.BlockSpec(memory_space=pl.ANY)] * anywhere
        + [pl.BlockSpec(memory_space=VMEM)] * (len(operands) - anywhere),
        out_specs=[pl.BlockSpec(memory_space=VMEM)] * len(outs),
        scratch_shapes=list(scratch),
        input_output_aliases=aliases,
        compiler_params=pltpu.CompilerParams(vmem_limit_bytes=32 * 2**20),
        cost_estimate=pl.CostEstimate(flops=cost, bytes_accessed=0, transcendentals=0),
    )(*operands)
    return result[0] if len(outs) == 1 else result


def body(features, occupancy, neighbours, kernel_one, kernel_two):
    side, width = features.shape[1], features.shape[4]
    rows, plane = side**3, side * side
    total = lax.axis_size(AXES)
    halves = [(i, i ^ 1) for i in range(total)]
    chips = total // 2
    first, second = chip_exchanges(chips)
    face = ((folded_rows(side, width), LANES), BF16)
    piece = ((rows // PARTS, width), BF16)
    wide = ((rows, width), F32)
    count = len(pieces(width))

    own = features.reshape(rows, width)
    mark = call(mark_kernel, (), [((8, LANES), F32)], cost=MARK_COST)
    mark, one_late = lax.optimization_barrier((mark, kernel_one))
    after = call(mark_kernel, (), [((8, LANES), F32)], cost=NEXT_COST)
    own_face, *own_parts = call(
        functools.partial(pack_kernel, side=side),
        (own, mark, after),
        [face] + [piece] * PARTS,
        [VMEM((count, rows, LANES), F32)],
        cost=PACK_COST,
    )
    table_other = lax.ppermute(neighbours, AXES, halves)
    other = [lax.ppermute(part, AXES, halves) for part in own_parts]
    far = lax.ppermute(own_face, AXES, first)

    def weights(kernel, late):
        flat = kernel.reshape((27,) + kernel.shape[3:])
        swapped = lax.ppermute(late.reshape(flat.shape), AXES, halves)
        return call(weights_kernel, (flat, swapped), [((3, 9 * width, width), BF16)])

    w_one, w_two = weights(kernel_one, one_late), weights(kernel_two, kernel_two)

    sums = ((count, rows, LANES), F32)
    near = ((count, 6 * 3 * (side + 2) * side, LANES), F32)
    masks = ((27 * 8, LANES), F32)

    def inside(layer, tables, here, there, w):
        counts = (len(tables), len(here), len(there))
        return call(
            functools.partial(
                inside_kernel, side=side, chips=chips, counts=counts, opening=layer == 0
            ),
            (*tables, *here, *there, w),
            [sums, near, masks],
            [
                VMEM((2, count, rows, LANES), F32),
                VMEM((count, 3 * 6 * plane, LANES), F32),
                VMEM((rows, 9 * width), BF16),
                SMEM((len(tables),) + neighbours.shape, jnp.int32),
                pltpu.SemaphoreType.DMA((len(tables),)),
            ],
            anywhere=len(tables),
        )

    planes = [
        VMEM((count, 6 * plane, LANES), F32),
        VMEM((6, 3, plane + 2 * side, width), BF16),
        VMEM((6, 3, plane, width), BF16),
    ]
    hidden_face, *hidden, _ = call(
        functools.partial(first_kernel, side=side),
        (far, w_one, *inside(0, (neighbours, table_other), own_parts, other, w_one)),
        [face] + [piece] * PARTS + [sums],
        planes,
        aliases={2: 1 + PARTS},
        cost=FIRST_COST,
    )
    hidden_other = [lax.ppermute(part, AXES, halves) for part in hidden]
    hidden_far = lax.ppermute(hidden_face, AXES, second)
    out, _ = call(
        functools.partial(second_kernel, side=side),
        (
            occupancy.reshape(1, 1),
            hidden_far,
            w_two,
            own,
            *inside(1, (neighbours,), hidden, hidden_other, w_two),
        ),
        [wide, sums],
        planes,
        aliases={4: 1},
    )
    return out.reshape((1, side, side, side, width))


def solution(mesh):
    return jax.shard_map(
        body,
        mesh=mesh,
        in_specs=(
            P(AXES, None, None, None, None),
            P(AXES),
            P(AXES, None),
            P(None, None, None, None, "wt"),
            P(None, None, None, None, "wt"),
        ),
        out_specs=P(AXES, None, None, None, None),
        check_vma=False,
    )
```

```python
import functools

import jax
import jax.numpy as jnp
from jax import lax
from jax.experimental import pallas as pl
from jax.experimental.pallas import tpu as pltpu
from jax.sharding import PartitionSpec as P

PARTS = 2
MARK_COST = 65 * 10**7
NEXT_COST = 30 * 10**7
PACK_COST = 4 * 10**9
FIRST_COST = 18 * 10**9
AXES = ("space", "wt")
VMEM = pltpu.VMEM
SMEM = pltpu.SMEM
LANES = 128
F32 = jnp.float32
BF16 = jnp.bfloat16


def pieces(width):
    return [
        (p, p * LANES, min(LANES, width - p * LANES)) for p in range(-(-width // LANES))
    ]


def fill(wide, base, value):
    rows, width = value.shape
    for p, lane, lanes in pieces(width):
        wide[p, pl.ds(base, rows), 0:lanes] = value[:, lane : lane + lanes]


def surface_rows(side):
    return side**3 - (side - 2) ** 3


def folded_shape(side, lanes):
    rows, folds = surface_rows(side), LANES // lanes
    short = rows // folds // 16 * 16
    return folds, short, rows - folds * short


def folded_rows(side, width):
    rows = 0
    for p, lane, lanes in pieces(width):
        folds, short, left = folded_shape(side, lanes)
        rows += surface_rows(side) if folds == 1 else short + left
    return -(-rows // 16) * 16


def folded_start(side, width):
    rows = surface_rows(side) * (width // LANES)
    for p, lane, lanes in pieces(width):
        if lanes < LANES:
            rows += folded_shape(side, lanes)[2]
    return -(-rows // 16) * 16


def pack_surface(wide, out_ref, side, width, change=lambda value: value):
    plane = side * side
    last = side - 1
    rows = surface_rows(side)
    start = folded_start(side, width)
    whole = []
    for p, lane, lanes in pieces(width):
        ref = wide.at[p]
        parts = [ref[pl.ds(0, plane), :], ref[pl.ds(last * plane, plane), :]]
        for y in (0, last):
            for x in range(1, last):
                parts.append(ref[pl.ds(x * plane + y * side, side), :])
        for z in (0, last):
            for x in range(1, last):
                at = x * plane + side + z
                parts.append(ref[pl.ds(at, side - 2, stride=side), :])
        value = change(jnp.concatenate(parts, axis=0))
        folds, count, left = folded_shape(side, lanes)
        if folds == 1:
            whole.append(value)
            continue
        whole.append(value[folds * count :])
        result = value[:count]
        position = lax.broadcasted_iota(jnp.int32, (count, LANES), 1)
        for n in range(1, folds):
            part = pltpu.roll(value[n * count : (n + 1) * count], n * lanes, axis=1)
            result = jnp.where(position >= n * lanes, part, result)
        out_ref[pl.ds(start, count), :] = result.astype(BF16)
    value = jnp.concatenate(whole, axis=0)
    if value.shape[0] < start:
        rest = jnp.zeros((start - value.shape[0], LANES), F32)
        value = jnp.concatenate([value, rest], axis=0)
    out_ref[pl.ds(0, start), :] = value.astype(BF16)


def spread_surface(packed_ref, faces, slot, side, width):
    plane = side * side
    inner = (side - 2) * side
    last = side - 1
    base = slot * 6 * plane
    rows = surface_rows(side)
    start = folded_start(side, width)
    whole = packed_ref[pl.ds(0, start), :].astype(F32)
    for p, lane, lanes in pieces(width):
        ref = faces.at[p]
        folds, count, left = folded_shape(side, lanes)
        if folds == 1:
            part = whole[p * rows : (p + 1) * rows]
        else:
            part = packed_ref[pl.ds(start, count), :].astype(F32)
            turned = [part] + [
                pltpu.roll(part, LANES - n * lanes, axis=1) for n in range(1, folds)
            ]
            turned.append(whole[p * rows : p * rows + left])
            part = jnp.concatenate(turned, axis=0)
        ref[pl.ds(base, 2 * plane), :] = part[: 2 * plane]
        row = 2 * plane
        for f in (2, 3):
            ref[pl.ds(base + f * plane + side, inner), :] = part[row : row + inner]
            row += inner
        for f in (4, 5):
            for x in range(1, last):
                at = base + f * plane + x * side + 1
                ref[pl.ds(at, side - 2), :] = part[row : row + side - 2]
                row += side - 2
        for end, x in ((0, 0), (1, last)):
            for f, y in ((2, 0), (3, last)):
                ref[pl.ds(base + f * plane + x * side, side), :] = ref[
                    pl.ds(base + end * plane + y * side, side), :
                ]
            for f, z in ((4, 0), (5, last)):
                ref[pl.ds(base + f * plane + x * side, side), :] = ref[
                    pl.ds(base + end * plane + z, side, stride=side), :
                ]
        for f, z in ((4, 0), (5, last)):
            for g, y in ((2, 0), (3, last)):
                ref[pl.ds(base + f * plane + y, side, stride=side), :] = ref[
                    pl.ds(base + g * plane + z, side, stride=side), :
                ]


def cut_surface(wide, faces, slot, side):
    plane = side * side
    last = side - 1
    base = slot * 6 * plane
    for p in range(wide.shape[0]):
        for n, x in enumerate((0, last)):
            faces[p, pl.ds(base + n * plane, plane), :] = wide[
                p, pl.ds(x * plane, plane), :
            ]
        for n, y in ((2, 0), (3, last)):
            for x in range(side):
                faces[p, pl.ds(base + n * plane + x * side, side), :] = wide[
                    p, pl.ds(x * plane + y * side, side), :
                ]
        for n, z in ((4, 0), (5, last)):
            faces[p, pl.ds(base + n * plane, plane), :] = wide.at[p][
                pl.ds(z, plane, stride=side), :
            ]


def mark_kernel(out_ref):
    out_ref[...] = jnp.zeros(out_ref.shape, out_ref.dtype)


def pack_kernel(x_ref, mark, after, out_ref, *refs, side):
    *pieces_out, wide = refs
    fill(wide, 0, x_ref[...].astype(F32))
    pack_surface(wide, out_ref, side, x_ref.shape[1])
    share(x_ref[...], pieces_out)


def share(value, refs):
    for n, ref in enumerate(refs):
        count = ref.shape[0]
        ref[...] = value[n * count : (n + 1) * count]


def weight_rows(width, tap):
    return [
        (lane, 9 * lane + tap * lanes, lanes) for _, lane, lanes in pieces(width)
    ]


def weights_kernel(own_ref, other_ref, out_ref):
    core = lax.axis_index("wt")
    taps, depth, both = own_ref.shape
    width = out_ref.shape[2]
    half = depth * (both // width)
    step = 16
    for tap in range(taps):
        rows = {}
        for channel, row, count in weight_rows(width, tap % 9):
            for n in range(0, count, step):
                rows[channel + n] = row + n
        for ref, place in ((own_ref, core), (other_ref, 1 - core)):
            for group in range(both // width):
                lane = group * width
                value = ref[tap, :, lane : lane + width]
                for n in range(0, depth, step):
                    at = group * depth + n
                    row = jnp.where(place == 0, rows[at], rows[at + half])
                    row = pl.multiple_of(row, step)
                    out_ref[tap // 9, pl.ds(row, step), :] = value[n : n + step]


def tap_weights(w, tap):
    third, tap = divmod(tap, 9)
    return jnp.concatenate(
        [w[third, pl.ds(row, count), :] for _, row, count in weight_rows(w.shape[2], tap)],
        axis=0,
    )


def shifts(middle, low, high, mask):
    side = middle.shape[1]
    return (
        pltpu.roll(jnp.where(mask == side - 1, low, middle), 1, axis=1),
        middle,
        pltpu.roll(jnp.where(mask == 0, high, middle), side - 1, axis=1),
    )


def turned_chip(chips):
    chip = lax.axis_index("space")
    return ((chip == 0) | (chip == chips - 1)).astype(jnp.int32)


def inside_kernel(*refs, side, chips, counts, opening):
    refs = list(refs)
    table_refs, extra, *sources = [[refs.pop(0) for _ in range(n)] for n in counts]
    w, total, near, masks, ends, wide, faces, lhs, tables, semaphores = refs
    copies = [
        pltpu.make_async_copy(ref, tables.at[n], semaphores.at[n])
        for n, ref in enumerate(table_refs)
    ]
    for copy in copies:
        copy.start()
    width = w.shape[2]
    plane = side * side
    turned = turned_chip(chips)
    home = 2 * lax.axis_index("space") + lax.axis_index("wt")
    other = home + 1 - 2 * lax.axis_index("wt")
    away = jnp.where(turned == 1, other, home)
    ids = (home, other) if opening else (away, home + other - away)
    for slot, parts in enumerate(sources):
        for n, part in enumerate(parts):
            fill(wide.at[slot], n * part.shape[0], part[...].astype(F32))
    mask = lax.broadcasted_iota(jnp.int32, (side, side, LANES), 1)
    nothing = jnp.zeros((side, side, LANES), F32)
    edge = jnp.zeros((1, side, LANES), F32)
    for p, lane, lanes in pieces(width):
        folds = LANES // lanes
        for x in range(side):
            middle = wide[turned, p, pl.ds(x * plane, plane), :]
            middle = middle.reshape(side, side, LANES)
            if folds > 1:
                position = lax.broadcasted_iota(jnp.int32, middle.shape, 2)
                for n in range(1, folds):
                    moved = pltpu.roll(middle, n * lanes, axis=2)
                    middle = jnp.where(position >= n * lanes, moved, middle)
            moved = shifts(middle, nothing, nothing, mask)
            taps = []
            for j in range(3):
                for k in range(3):
                    value = moved[k]
                    if j == 0:
                        value = jnp.concatenate([edge, value[: side - 1]], axis=0)
                    elif j == 2:
                        value = jnp.concatenate([value[1:], edge], axis=0)
                    taps.append(value.reshape(plane, LANES))
            for t in range(0, 9, folds):
                value = taps[t]
                used = min(folds, 9 - t)
                for n in range(1, used):
                    position = lax.broadcasted_iota(jnp.int32, value.shape, 1)
                    value = jnp.where(position >= n * lanes, taps[t + n], value)
                at = 9 * lane + t * lanes
                lhs[pl.ds(x * plane, plane), at : at + used * lanes] = value[
                    :, : used * lanes
                ].astype(BF16)
    for i in (1, 0, 2):
        first, source, count = (1, 0, 0)[i], (0, 0, 1)[i], side - (i != 1)
        acc = jnp.dot(
            lhs[pl.ds(source * plane, count * plane), :],
            w[i],
            preferred_element_type=F32,
        )
        for p, lane, lanes in pieces(width):
            part = acc[:, lane : lane + lanes]
            place = pl.ds(first * plane, count * plane)
            if i == 1:
                for ref in extra:
                    part = part + ref[:, lane : lane + lanes].astype(F32)
                total[p, place, 0:lanes] = part
            else:
                total[p, place, 0:lanes] += part
    for p in range(total.shape[0]):
        for n, z in enumerate((0, side - 1)):
            ends[p, pl.ds(n * plane, plane), :] = total.at[p][
                pl.ds(z, plane, stride=side), :
            ]
    fill(faces, 0, jnp.zeros((6 * plane, width), F32))
    for slot in range(2):
        cut_surface(wide.at[slot], faces, slot + 1, side)
    for copy in copies:
        copy.wait()
    row = turned if opening else 0
    entries = [tables[row, 0, t] for t in range(27)]
    choose_near(entries, ids, faces, near, masks, side)


def borders(side):
    last = side - 1
    for group in range(6):
        axis, up = divmod(group, 2)
        face = 2 * axis + 1 - up
        sign = 2 * up - 1
        for to, count, row, b in (
            (0, 1, last * side, -1),
            (1, side, 0, 0),
            (side + 1, 1, 0, 1),
        ):
            offsets = {}
            for c in (-1, 0, 1):
                if axis == 0:
                    offsets[c] = (sign, b, c)
                elif axis == 1 and b == 0:
                    offsets[c] = (0, sign, c)
                elif axis == 2 and b == 0 and c == 0:
                    offsets[c] = (0, 0, sign)
            yield group, to, count, row, face, offsets


def entry(offset):
    a, b, c = offset
    return 9 * (a + 1) + 3 * (b + 1) + c + 1


def choose_near(entries, ids, faces, near, masks, side):
    plane = side * side

    def slot(n):
        here = jnp.where(n == ids[0], 1, jnp.where(n == ids[1], 2, 3))
        return jnp.where(n < 0, 0, here)

    slots = [slot(n) for n in entries]
    for t, value in enumerate(slots):
        flag = (value > 0 if t == 13 else value == 3).astype(F32)
        masks[pl.ds(8 * t, 8), :] = jnp.full((8, LANES), flag, F32)
    for group, to, count, row, face, offsets in borders(side):
        for c, offset in offsets.items():
            value = slots[entry(offset)]
            source = jnp.where(value == 3, 0, value)
            start = pl.multiple_of((source * 6 + face) * plane + row, side)
            place = pl.ds(((3 * group + c + 1) * (side + 2) + to) * side, count * side)
            for p in range(faces.shape[0]):
                near[p, place, :] = faces[p, pl.ds(start, count * side), :]


def add_outside(far, w, near, masks, ends, total, faces, even, odd, side):
    width = w.shape[2]
    plane = side * side
    last = side - 1
    spread_surface(far, faces, 0, side, width)
    mask = lax.broadcasted_iota(jnp.int32, (side, side, LANES), 1)
    for group, to, count, row, face, offsets in borders(side):
        for p, lane, lanes in pieces(width):
            place = pl.ds(to * side, count * side)
            if not offsets:
                blank = jnp.zeros((3, side, lanes), BF16)
                even[group, :, place, lane : lane + lanes] = blank
                continue

            def chunk(c):
                if c not in offsets:
                    return jnp.zeros((count, side, LANES), F32)
                away = masks[pl.ds(8 * entry(offsets[c]), 8), :] > 0
                at = ((3 * group + c + 1) * (side + 2) + to) * side
                afar = faces[p, pl.ds(face * plane + row, count * side), :]
                here = near[p, pl.ds(at, count * side), :]
                shape = (count, side, LANES)
                return jnp.where(
                    jnp.broadcast_to(away[None], shape),
                    afar.reshape(shape),
                    here.reshape(shape),
                )

            moved = shifts(chunk(0), chunk(-1), chunk(1), mask[:count])
            for k, value in enumerate(moved):
                value = value.reshape(count * side, LANES)[:, :lanes]
                if count == side:
                    odd[group, k, :, lane : lane + lanes] = value.astype(BF16)
                even[group, k, place, lane : lane + lanes] = value.astype(BF16)

    sums = [None] * 6
    for i in range(3):
        for j in range(3):
            for k in range(3):
                parts, groups = [], []
                for axis, tap, chunk, shift in ((0, i, j, k), (1, j, i, k), (2, k, i, j)):
                    if tap == 1:
                        continue
                    group = 2 * axis + tap // 2
                    if chunk == 1:
                        parts.append(odd[group, shift])
                    else:
                        parts.append(
                            even[group, shift, chunk * side : chunk * side + plane]
                        )
                    groups.append(group)
                if not parts:
                    continue
                product = jnp.dot(
                    jnp.concatenate(parts, axis=0),
                    tap_weights(w, 9 * i + 3 * j + k),
                    preferred_element_type=F32,
                )
                for n, group in enumerate(groups):
                    part = product[n * plane : (n + 1) * plane]
                    sums[group] = part if sums[group] is None else sums[group] + part

    for p, lane, lanes in pieces(width):
        ref = total.at[p]
        part = [value[:, lane : lane + lanes] for value in sums]
        if lanes < LANES:
            pad = jnp.zeros((plane, LANES - lanes), F32)
            part = [jnp.concatenate([value, pad], axis=1) for value in part]
        for up, z in ((0, 0), (1, last)):
            line = ends[p, pl.ds(up * plane, plane), :]
            ref[pl.ds(z, plane, stride=side), :] = line + part[4 + up]
        for up, x in ((0, 0), (1, last)):
            ref[pl.ds(x * plane, plane), :] += part[up]
        for up, y in ((0, 0), (1, last)):
            for x in range(side):
                ref[pl.ds(x * plane + y * side, side), :] += part[2 + up][
                    x * side : (x + 1) * side
                ]


def first_kernel(far, w, total_in, near, masks, ends, surface, *refs, side):
    *outs, total, faces, even, odd = refs
    add_outside(far, w, near, masks, ends, total, faces, even, odd, side)
    active = masks[pl.ds(8 * 13, 1), :]

    def change(value):
        return jnp.maximum(value, 0.0) * active[:, : value.shape[1]]

    pack_surface(total, surface, side, w.shape[2], change)
    for p, lane, lanes in pieces(w.shape[2]):
        for n, out in enumerate(outs):
            count = out.shape[0]
            value = change(total[p, pl.ds(n * count, count), 0:lanes])
            out[:, lane : lane + lanes] = value.astype(BF16)


def second_kernel(
    occupancy, far, w, total_in, near, masks, ends, out, total, faces, even, odd, *, side
):
    add_outside(far, w, near, masks, ends, total, faces, even, odd, side)
    active = occupancy[...].astype(F32)
    for p, lane, lanes in pieces(w.shape[2]):
        value = jnp.maximum(total[p, :, 0:lanes], 0.0)
        out[:, lane : lane + lanes] = value * active


def chip_exchanges(chips):
    def end(chip):
        return int(chip in (0, chips - 1))

    last = 2 * chips - 1
    first, second = [(0, 1), (last, last - 1)], [(1, 0), (last - 1, last)]
    for c in range(chips - 1):
        up, down = 2 * c, 2 * (c + 1)
        first.append((up + 1, down + end(c + 1)))
        first.append((down, up + 1 - end(c)))
        second.append((up + 1 - end(c), down))
        second.append((down + end(c + 1), up + 1))
    return first, second


def call(kernel, operands, outs, scratch=(), anywhere=0, cost=0, aliases={}):
    outs = [jax.ShapeDtypeStruct(shape, kind) for shape, kind in outs]
    result = pl.pallas_call(
        kernel,
        out_shape=outs,
        in_specs=[pl.BlockSpec(memory_space=pl.ANY)] * anywhere
        + [pl.BlockSpec(memory_space=VMEM)] * (len(operands) - anywhere),
        out_specs=[pl.BlockSpec(memory_space=VMEM)] * len(outs),
        scratch_shapes=list(scratch),
        input_output_aliases=aliases,
        compiler_params=pltpu.CompilerParams(vmem_limit_bytes=32 * 2**20),
        cost_estimate=pl.CostEstimate(flops=cost, bytes_accessed=0, transcendentals=0),
    )(*operands)
    return result[0] if len(outs) == 1 else result


def body(features, occupancy, neighbours, kernel_one, kernel_two):
    side, width = features.shape[1], features.shape[4]
    rows, plane = side**3, side * side
    total = lax.axis_size(AXES)
    halves = [(i, i ^ 1) for i in range(total)]
    chips = total // 2
    first, second = chip_exchanges(chips)
    face = ((folded_rows(side, width), LANES), BF16)
    piece = ((rows // PARTS, width), BF16)
    wide = ((rows, width), F32)
    count = len(pieces(width))

    own = features.reshape(rows, width)
    mark = call(mark_kernel, (), [((8, LANES), F32)], cost=MARK_COST)
    mark, one_late = lax.optimization_barrier((mark, kernel_one))
    after = call(mark_kernel, (), [((8, LANES), F32)], cost=NEXT_COST)
    own_face, *own_parts = call(
        functools.partial(pack_kernel, side=side),
        (own, mark, after),
        [face] + [piece] * PARTS,
        [VMEM((count, rows, LANES), F32)],
        cost=PACK_COST,
    )
    table_other = lax.ppermute(neighbours, AXES, halves)
    other = [lax.ppermute(part, AXES, halves) for part in own_parts]
    far = lax.ppermute(own_face, AXES, first)

    def weights(kernel, late):
        flat = kernel.reshape((27,) + kernel.shape[3:])
        swapped = lax.ppermute(late.reshape(flat.shape), AXES, halves)
        return call(weights_kernel, (flat, swapped), [((3, 9 * width, width), BF16)])

    w_one, w_two = weights(kernel_one, one_late), weights(kernel_two, kernel_two)

    sums = ((count, rows, LANES), F32)
    near = ((count, 6 * 3 * (side + 2) * side, LANES), F32)
    masks = ((27 * 8, LANES), F32)
    ends = ((count, 2 * plane, LANES), F32)

    def inside(layer, tables, extra, here, there, w):
        counts = (len(tables), len(extra), len(here), len(there))
        return call(
            functools.partial(
                inside_kernel, side=side, chips=chips, counts=counts, opening=layer == 0
            ),
            (*tables, *extra, *here, *there, w),
            [sums, near, masks, ends],
            [
                VMEM((2, count, rows, LANES), F32),
                VMEM((count, 3 * 6 * plane, LANES), F32),
                VMEM((rows, 9 * width), BF16),
                SMEM((len(tables),) + neighbours.shape, jnp.int32),
                pltpu.SemaphoreType.DMA((len(tables),)),
            ],
            anywhere=len(tables),
        )

    planes = [
        VMEM((count, 6 * plane, LANES), F32),
        VMEM((6, 3, plane + 2 * side, width), BF16),
        VMEM((6, 3, plane, width), BF16),
    ]
    hidden_face, *hidden, _ = call(
        functools.partial(first_kernel, side=side),
        (far, w_one, *inside(0, (neighbours, table_other), (), own_parts, other, w_one)),
        [face] + [piece] * PARTS + [sums],
        planes,
        aliases={2: 1 + PARTS},
        cost=FIRST_COST,
    )
    hidden_other = [lax.ppermute(part, AXES, halves) for part in hidden]
    hidden_far = lax.ppermute(hidden_face, AXES, second)
    out, _ = call(
        functools.partial(second_kernel, side=side),
        (
            occupancy.reshape(1, 1),
            hidden_far,
            w_two,
            *inside(1, (neighbours,), (own,), hidden, hidden_other, w_two),
        ),
        [wide, sums],
        planes,
        aliases={3: 1},
    )
    return out.reshape((1, side, side, side, width))


def solution(mesh):
    return jax.shard_map(
        body,
        mesh=mesh,
        in_specs=(
            P(AXES, None, None, None, None),
            P(AXES),
            P(AXES, None),
            P(None, None, None, None, "wt"),
            P(None, None, None, None, "wt"),
        ),
        out_specs=P(AXES, None, None, None, None),
        check_vma=False,
    )
```

```python
import functools

import jax
import jax.numpy as jnp
from jax import lax
from jax.experimental import pallas as pl
from jax.experimental.pallas import tpu as pltpu
from jax.sharding import PartitionSpec as P

PARTS = 2
MARK_COST = 65 * 10**7
NEXT_COST = 30 * 10**7
PACK_COST = 4 * 10**9
FIRST_COST = 18 * 10**9
AXES = ("space", "wt")
VMEM = pltpu.VMEM
SMEM = pltpu.SMEM
LANES = 128
F32 = jnp.float32
BF16 = jnp.bfloat16


def pieces(width):
    return [
        (p, p * LANES, min(LANES, width - p * LANES)) for p in range(-(-width // LANES))
    ]


def fill(wide, base, value):
    rows, width = value.shape
    for p, lane, lanes in pieces(width):
        wide[p, pl.ds(base, rows), 0:lanes] = value[:, lane : lane + lanes]


def surface_rows(side):
    return side**3 - (side - 2) ** 3


def folded_shape(side, lanes):
    rows, folds = surface_rows(side), LANES // lanes
    short = rows // folds // 16 * 16
    return folds, short, rows - folds * short


def folded_rows(side, width):
    rows = 0
    for p, lane, lanes in pieces(width):
        folds, short, left = folded_shape(side, lanes)
        rows += surface_rows(side) if folds == 1 else short + left
    return -(-rows // 16) * 16


def folded_start(side, width):
    rows = surface_rows(side) * (width // LANES)
    for p, lane, lanes in pieces(width):
        if lanes < LANES:
            rows += folded_shape(side, lanes)[2]
    return -(-rows // 16) * 16


def pack_surface(wide, out_ref, side, width, change=lambda value: value):
    plane = side * side
    last = side - 1
    rows = surface_rows(side)
    start = folded_start(side, width)
    whole = []
    for p, lane, lanes in pieces(width):
        ref = wide.at[p]
        parts = [ref[pl.ds(0, plane), :], ref[pl.ds(last * plane, plane), :]]
        for y in (0, last):
            for x in range(1, last):
                parts.append(ref[pl.ds(x * plane + y * side, side), :])
        for z in (0, last):
            for x in range(1, last):
                at = x * plane + side + z
                parts.append(ref[pl.ds(at, side - 2, stride=side), :])
        value = change(jnp.concatenate(parts, axis=0))
        folds, count, left = folded_shape(side, lanes)
        if folds == 1:
            whole.append(value)
            continue
        whole.append(value[folds * count :])
        result = value[:count]
        position = lax.broadcasted_iota(jnp.int32, (count, LANES), 1)
        for n in range(1, folds):
            part = pltpu.roll(value[n * count : (n + 1) * count], n * lanes, axis=1)
            result = jnp.where(position >= n * lanes, part, result)
        out_ref[pl.ds(start, count), :] = result.astype(BF16)
    value = jnp.concatenate(whole, axis=0)
    if value.shape[0] < start:
        rest = jnp.zeros((start - value.shape[0], LANES), F32)
        value = jnp.concatenate([value, rest], axis=0)
    out_ref[pl.ds(0, start), :] = value.astype(BF16)


def spread_surface(packed_ref, faces, slot, side, width):
    plane = side * side
    inner = (side - 2) * side
    last = side - 1
    base = slot * 6 * plane
    rows = surface_rows(side)
    start = folded_start(side, width)
    whole = packed_ref[pl.ds(0, start), :].astype(F32)
    for p, lane, lanes in pieces(width):
        ref = faces.at[p]
        folds, count, left = folded_shape(side, lanes)
        if folds == 1:
            part = whole[p * rows : (p + 1) * rows]
        else:
            part = packed_ref[pl.ds(start, count), :].astype(F32)
            turned = [part] + [
                pltpu.roll(part, LANES - n * lanes, axis=1) for n in range(1, folds)
            ]
            turned.append(whole[p * rows : p * rows + left])
            part = jnp.concatenate(turned, axis=0)
        ref[pl.ds(base, 2 * plane), :] = part[: 2 * plane]
        row = 2 * plane
        for f in (2, 3):
            ref[pl.ds(base + f * plane + side, inner), :] = part[row : row + inner]
            row += inner
        for f in (4, 5):
            for x in range(1, last):
                at = base + f * plane + x * side + 1
                ref[pl.ds(at, side - 2), :] = part[row : row + side - 2]
                row += side - 2
        for end, x in ((0, 0), (1, last)):
            for f, y in ((2, 0), (3, last)):
                ref[pl.ds(base + f * plane + x * side, side), :] = ref[
                    pl.ds(base + end * plane + y * side, side), :
                ]
            for f, z in ((4, 0), (5, last)):
                ref[pl.ds(base + f * plane + x * side, side), :] = ref[
                    pl.ds(base + end * plane + z, side, stride=side), :
                ]
        for f, z in ((4, 0), (5, last)):
            for g, y in ((2, 0), (3, last)):
                ref[pl.ds(base + f * plane + y, side, stride=side), :] = ref[
                    pl.ds(base + g * plane + z, side, stride=side), :
                ]


def cut_surface(wide, faces, slot, side):
    plane = side * side
    last = side - 1
    base = slot * 6 * plane
    for p in range(wide.shape[0]):
        for n, x in enumerate((0, last)):
            faces[p, pl.ds(base + n * plane, plane), :] = wide[
                p, pl.ds(x * plane, plane), :
            ]
        for n, y in ((2, 0), (3, last)):
            for x in range(side):
                faces[p, pl.ds(base + n * plane + x * side, side), :] = wide[
                    p, pl.ds(x * plane + y * side, side), :
                ]
        for n, z in ((4, 0), (5, last)):
            faces[p, pl.ds(base + n * plane, plane), :] = wide.at[p][
                pl.ds(z, plane, stride=side), :
            ]


def mark_kernel(out_ref):
    out_ref[...] = jnp.zeros(out_ref.shape, out_ref.dtype)


def pack_kernel(x_ref, mark, after, out_ref, *refs, side):
    *pieces_out, wide = refs
    fill(wide, 0, x_ref[...].astype(F32))
    pack_surface(wide, out_ref, side, x_ref.shape[1])
    share(x_ref[...], pieces_out)


def share(value, refs):
    for n, ref in enumerate(refs):
        count = ref.shape[0]
        ref[...] = value[n * count : (n + 1) * count]


def weight_rows(width, tap):
    return [
        (lane, 9 * lane + tap * lanes, lanes) for _, lane, lanes in pieces(width)
    ]


def weights_kernel(own_ref, other_ref, out_ref):
    core = lax.axis_index("wt")
    taps, depth, both = own_ref.shape
    width = out_ref.shape[2]
    half = depth * (both // width)
    step = 16
    for tap in range(taps):
        rows = {}
        for channel, row, count in weight_rows(width, tap % 9):
            for n in range(0, count, step):
                rows[channel + n] = row + n
        for ref, place in ((own_ref, core), (other_ref, 1 - core)):
            for group in range(both // width):
                lane = group * width
                value = ref[tap, :, lane : lane + width]
                for n in range(0, depth, step):
                    at = group * depth + n
                    row = jnp.where(place == 0, rows[at], rows[at + half])
                    row = pl.multiple_of(row, step)
                    out_ref[tap // 9, pl.ds(row, step), :] = value[n : n + step]


def tap_weights(w, tap):
    third, tap = divmod(tap, 9)
    return jnp.concatenate(
        [w[third, pl.ds(row, count), :] for _, row, count in weight_rows(w.shape[2], tap)],
        axis=0,
    )


def shifts(middle, low, high, mask):
    side = middle.shape[1]
    return (
        pltpu.roll(jnp.where(mask == side - 1, low, middle), 1, axis=1),
        middle,
        pltpu.roll(jnp.where(mask == 0, high, middle), side - 1, axis=1),
    )


def turned_chip(chips):
    chip = lax.axis_index("space")
    return ((chip == 0) | (chip == chips - 1)).astype(jnp.int32)


def inside_kernel(*refs, side, chips, counts, opening):
    refs = list(refs)
    table_refs, extra, *sources = [[refs.pop(0) for _ in range(n)] for n in counts]
    w, total, near, masks, ends, wide, faces, lhs, tables, semaphores = refs
    copies = [
        pltpu.make_async_copy(ref, tables.at[n], semaphores.at[n])
        for n, ref in enumerate(table_refs)
    ]
    for copy in copies:
        copy.start()
    width = w.shape[2]
    plane = side * side
    turned = turned_chip(chips)
    home = 2 * lax.axis_index("space") + lax.axis_index("wt")
    other = home + 1 - 2 * lax.axis_index("wt")
    away = jnp.where(turned == 1, other, home)
    ids = (home, other) if opening else (away, home + other - away)
    for slot, parts in enumerate(sources):
        for n, part in enumerate(parts):
            fill(wide.at[slot], n * part.shape[0], part[...].astype(F32))
    mask = lax.broadcasted_iota(jnp.int32, (side, side, LANES), 1)
    nothing = jnp.zeros((side, side, LANES), F32)
    edge = jnp.zeros((1, side, LANES), F32)
    for p, lane, lanes in pieces(width):
        folds = LANES // lanes
        for x in range(side):
            middle = wide[turned, p, pl.ds(x * plane, plane), :]
            middle = middle.reshape(side, side, LANES)
            if folds > 1:
                position = lax.broadcasted_iota(jnp.int32, middle.shape, 2)
                for n in range(1, folds):
                    moved = pltpu.roll(middle, n * lanes, axis=2)
                    middle = jnp.where(position >= n * lanes, moved, middle)
            moved = shifts(middle, nothing, nothing, mask)
            taps = []
            for j in range(3):
                for k in range(3):
                    value = moved[k]
                    if j == 0:
                        value = jnp.concatenate([edge, value[: side - 1]], axis=0)
                    elif j == 2:
                        value = jnp.concatenate([value[1:], edge], axis=0)
                    taps.append(value.reshape(plane, LANES))
            for t in range(0, 9, folds):
                value = taps[t]
                used = min(folds, 9 - t)
                for n in range(1, used):
                    position = lax.broadcasted_iota(jnp.int32, value.shape, 1)
                    value = jnp.where(position >= n * lanes, taps[t + n], value)
                at = 9 * lane + t * lanes
                lhs[pl.ds(x * plane, plane), at : at + used * lanes] = value[
                    :, : used * lanes
                ].astype(BF16)
    for i in (1, 0, 2):
        first, source, count = (1, 0, 0)[i], (0, 0, 1)[i], side - (i != 1)
        acc = jnp.dot(
            lhs[pl.ds(source * plane, count * plane), :],
            w[i],
            preferred_element_type=F32,
        )
        for p, lane, lanes in pieces(width):
            part = acc[:, lane : lane + lanes]
            place = pl.ds(first * plane, count * plane)
            if i == 1:
                for ref in extra:
                    part = part + ref[:, lane : lane + lanes].astype(F32)
                total[p, place, 0:lanes] = part
            else:
                total[p, place, 0:lanes] += part
    for p in range(total.shape[0]):
        for n, z in enumerate((0, side - 1)):
            ends[p, pl.ds(n * plane, plane), :] = total.at[p][
                pl.ds(z, plane, stride=side), :
            ]
    fill(faces, 0, jnp.zeros((6 * plane, width), F32))
    for slot in range(2):
        cut_surface(wide.at[slot], faces, slot + 1, side)
    for copy in copies:
        copy.wait()
    row = turned if opening else 0
    entries = [tables[row, 0, t] for t in range(27)]
    choose_near(entries, ids, faces, near, masks, side)


def borders(side):
    last = side - 1
    for group in range(6):
        axis, up = divmod(group, 2)
        face = 2 * axis + 1 - up
        sign = 2 * up - 1
        for to, count, row, b in (
            (0, 1, last * side, -1),
            (1, side, 0, 0),
            (side + 1, 1, 0, 1),
        ):
            offsets = {}
            for c in (-1, 0, 1):
                if axis == 0:
                    offsets[c] = (sign, b, c)
                elif axis == 1 and b == 0:
                    offsets[c] = (0, sign, c)
                elif axis == 2 and b == 0 and c == 0:
                    offsets[c] = (0, 0, sign)
            yield group, to, count, row, face, offsets


def entry(offset):
    a, b, c = offset
    return 9 * (a + 1) + 3 * (b + 1) + c + 1


def choose_near(entries, ids, faces, near, masks, side):
    plane = side * side

    def slot(n):
        here = jnp.where(n == ids[0], 1, jnp.where(n == ids[1], 2, 3))
        return jnp.where(n < 0, 0, here)

    slots = [slot(n) for n in entries]
    for t, value in enumerate(slots):
        flag = (value > 0 if t == 13 else value == 3).astype(F32)
        masks[pl.ds(8 * t, 8), :] = jnp.full((8, LANES), flag, F32)
    for group, to, count, row, face, offsets in borders(side):
        for c, offset in offsets.items():
            value = slots[entry(offset)]
            source = jnp.where(value == 3, 0, value)
            start = pl.multiple_of((source * 6 + face) * plane + row, side)
            place = pl.ds(((3 * group + c + 1) * (side + 2) + to) * side, count * side)
            for p in range(faces.shape[0]):
                near[p, place, :] = faces[p, pl.ds(start, count * side), :]


def add_outside(far, w, near, masks, ends, total, faces, even, odd, side, finish=None):
    width = w.shape[2]
    plane = side * side
    last = side - 1
    spread_surface(far, faces, 0, side, width)
    mask = lax.broadcasted_iota(jnp.int32, (side, side, LANES), 1)
    for group, to, count, row, face, offsets in borders(side):
        for p, lane, lanes in pieces(width):
            place = pl.ds(to * side, count * side)
            if not offsets:
                blank = jnp.zeros((3, side, lanes), BF16)
                even[group, :, place, lane : lane + lanes] = blank
                continue

            def chunk(c):
                if c not in offsets:
                    return jnp.zeros((count, side, LANES), F32)
                away = masks[pl.ds(8 * entry(offsets[c]), 8), :] > 0
                at = ((3 * group + c + 1) * (side + 2) + to) * side
                afar = faces[p, pl.ds(face * plane + row, count * side), :]
                here = near[p, pl.ds(at, count * side), :]
                shape = (count, side, LANES)
                return jnp.where(
                    jnp.broadcast_to(away[None], shape),
                    afar.reshape(shape),
                    here.reshape(shape),
                )

            moved = shifts(chunk(0), chunk(-1), chunk(1), mask[:count])
            for k, value in enumerate(moved):
                value = value.reshape(count * side, LANES)[:, :lanes]
                if count == side:
                    odd[group, k, :, lane : lane + lanes] = value.astype(BF16)
                even[group, k, place, lane : lane + lanes] = value.astype(BF16)

    sums = [None] * 6
    for i in range(3):
        for j in range(3):
            for k in range(3):
                parts, groups = [], []
                for axis, tap, chunk, shift in ((0, i, j, k), (1, j, i, k), (2, k, i, j)):
                    if tap == 1:
                        continue
                    group = 2 * axis + tap // 2
                    if chunk == 1:
                        parts.append(odd[group, shift])
                    else:
                        parts.append(
                            even[group, shift, chunk * side : chunk * side + plane]
                        )
                    groups.append(group)
                if not parts:
                    continue
                product = jnp.dot(
                    jnp.concatenate(parts, axis=0),
                    tap_weights(w, 9 * i + 3 * j + k),
                    preferred_element_type=F32,
                )
                for n, group in enumerate(groups):
                    part = product[n * plane : (n + 1) * plane]
                    sums[group] = part if sums[group] is None else sums[group] + part

    for p, lane, lanes in pieces(width):
        ref = total.at[p]
        part = [value[:, lane : lane + lanes] for value in sums]
        if lanes < LANES:
            pad = jnp.zeros((plane, LANES - lanes), F32)
            part = [jnp.concatenate([value, pad], axis=1) for value in part]
        for up, z in ((0, 0), (1, last)):
            line = ends[p, pl.ds(up * plane, plane), :]
            ref[pl.ds(z, plane, stride=side), :] = line + part[4 + up]
        for up, x in ((0, 0), (1, last)):
            ref[pl.ds(x * plane, plane), :] += part[up]
        for up, y in ((0, 0), (1, last)):
            for x in range(side):
                ref[pl.ds(x * plane + y * side, side), :] += part[2 + up][
                    x * side : (x + 1) * side
                ]
        if finish is not None:
            finish(p, lane, lanes)


def first_kernel(far, w, total_in, near, masks, ends, surface, *refs, side):
    *outs, total, faces, even, odd = refs
    add_outside(far, w, near, masks, ends, total, faces, even, odd, side)
    active = masks[pl.ds(8 * 13, 1), :]

    def change(value):
        return jnp.maximum(value, 0.0) * active[:, : value.shape[1]]

    pack_surface(total, surface, side, w.shape[2], change)
    for p, lane, lanes in pieces(w.shape[2]):
        for n, out in enumerate(outs):
            count = out.shape[0]
            value = change(total[p, pl.ds(n * count, count), 0:lanes])
            out[:, lane : lane + lanes] = value.astype(BF16)


def second_kernel(
    occupancy, far, w, total_in, near, masks, ends, out, total, *refs, side
):
    faces, even, odd, block, semaphores = refs
    active = occupancy[...].astype(F32)
    copies = []

    def finish(p, lane, lanes):
        value = jnp.maximum(total[p, :, 0:lanes], 0.0)
        block[:, lane : lane + lanes] = value * active
        place = (slice(None), pl.ds(lane, lanes))
        copies.append(
            pltpu.make_async_copy(block.at[place], out.at[place], semaphores.at[p])
        )
        copies[-1].start()

    add_outside(far, w, near, masks, ends, total, faces, even, odd, side, finish)
    for copy in copies:
        copy.wait()


def chip_exchanges(chips):
    def end(chip):
        return int(chip in (0, chips - 1))

    last = 2 * chips - 1
    first, second = [(0, 1), (last, last - 1)], [(1, 0), (last - 1, last)]
    for c in range(chips - 1):
        up, down = 2 * c, 2 * (c + 1)
        first.append((up + 1, down + end(c + 1)))
        first.append((down, up + 1 - end(c)))
        second.append((up + 1 - end(c), down))
        second.append((down + end(c + 1), up + 1))
    return first, second


def call(kernel, operands, outs, scratch=(), anywhere=0, cost=0, aliases={}, result_space=VMEM):
    outs = [jax.ShapeDtypeStruct(shape, kind) for shape, kind in outs]
    result = pl.pallas_call(
        kernel,
        out_shape=outs,
        in_specs=[pl.BlockSpec(memory_space=pl.ANY)] * anywhere
        + [pl.BlockSpec(memory_space=VMEM)] * (len(operands) - anywhere),
        out_specs=[pl.BlockSpec(memory_space=result_space)]
        + [pl.BlockSpec(memory_space=VMEM)] * (len(outs) - 1),
        scratch_shapes=list(scratch),
        input_output_aliases=aliases,
        compiler_params=pltpu.CompilerParams(vmem_limit_bytes=32 * 2**20),
        cost_estimate=pl.CostEstimate(flops=cost, bytes_accessed=0, transcendentals=0),
    )(*operands)
    return result[0] if len(outs) == 1 else result


def body(features, occupancy, neighbours, kernel_one, kernel_two):
    side, width = features.shape[1], features.shape[4]
    rows, plane = side**3, side * side
    total = lax.axis_size(AXES)
    halves = [(i, i ^ 1) for i in range(total)]
    chips = total // 2
    first, second = chip_exchanges(chips)
    face = ((folded_rows(side, width), LANES), BF16)
    piece = ((rows // PARTS, width), BF16)
    wide = ((rows, width), F32)
    count = len(pieces(width))

    own = features.reshape(rows, width)
    mark = call(mark_kernel, (), [((8, LANES), F32)], cost=MARK_COST)
    mark, one_late = lax.optimization_barrier((mark, kernel_one))
    after = call(mark_kernel, (), [((8, LANES), F32)], cost=NEXT_COST)
    own_face, *own_parts = call(
        functools.partial(pack_kernel, side=side),
        (own, mark, after),
        [face] + [piece] * PARTS,
        [VMEM((count, rows, LANES), F32)],
        cost=PACK_COST,
    )
    table_other = lax.ppermute(neighbours, AXES, halves)
    other = [lax.ppermute(part, AXES, halves) for part in own_parts]
    far = lax.ppermute(own_face, AXES, first)

    def weights(kernel, late):
        flat = kernel.reshape((27,) + kernel.shape[3:])
        swapped = lax.ppermute(late.reshape(flat.shape), AXES, halves)
        return call(weights_kernel, (flat, swapped), [((3, 9 * width, width), BF16)])

    w_one, w_two = weights(kernel_one, one_late), weights(kernel_two, kernel_two)

    sums = ((count, rows, LANES), F32)
    near = ((count, 6 * 3 * (side + 2) * side, LANES), F32)
    masks = ((27 * 8, LANES), F32)
    ends = ((count, 2 * plane, LANES), F32)

    def inside(layer, tables, extra, here, there, w):
        counts = (len(tables), len(extra), len(here), len(there))
        return call(
            functools.partial(
                inside_kernel, side=side, chips=chips, counts=counts, opening=layer == 0
            ),
            (*tables, *extra, *here, *there, w),
            [sums, near, masks, ends],
            [
                VMEM((2, count, rows, LANES), F32),
                VMEM((count, 3 * 6 * plane, LANES), F32),
                VMEM((rows, 9 * width), BF16),
                SMEM((len(tables),) + neighbours.shape, jnp.int32),
                pltpu.SemaphoreType.DMA((len(tables),)),
            ],
            anywhere=len(tables),
        )

    planes = [
        VMEM((count, 6 * plane, LANES), F32),
        VMEM((6, 3, plane + 2 * side, width), BF16),
        VMEM((6, 3, plane, width), BF16),
    ]
    hidden_face, *hidden, _ = call(
        functools.partial(first_kernel, side=side),
        (far, w_one, *inside(0, (neighbours, table_other), (), own_parts, other, w_one)),
        [face] + [piece] * PARTS + [sums],
        planes,
        aliases={2: 1 + PARTS},
        cost=FIRST_COST,
    )
    hidden_other = [lax.ppermute(part, AXES, halves) for part in hidden]
    hidden_far = lax.ppermute(hidden_face, AXES, second)
    out, _ = call(
        functools.partial(second_kernel, side=side),
        (
            occupancy.reshape(1, 1),
            hidden_far,
            w_two,
            *inside(1, (neighbours,), (own,), hidden, hidden_other, w_two),
        ),
        [wide, sums],
        planes + [VMEM((rows, width), F32), pltpu.SemaphoreType.DMA((count,))],
        result_space=pl.ANY,
        aliases={3: 1},
    )
    return out.reshape((1, side, side, side, width))


def solution(mesh):
    return jax.shard_map(
        body,
        mesh=mesh,
        in_specs=(
            P(AXES, None, None, None, None),
            P(AXES),
            P(AXES, None),
            P(None, None, None, None, "wt"),
            P(None, None, None, None, "wt"),
        ),
        out_specs=P(AXES, None, None, None, None),
        check_vma=False,
    )
```

```python
import functools

import jax
import jax.numpy as jnp
from jax import lax
from jax.experimental import pallas as pl
from jax.experimental.pallas import tpu as pltpu
from jax.sharding import PartitionSpec as P

PARTS = 2
MARK_COST = 65 * 10**7
NEXT_COST = 30 * 10**7
PACK_COST = 4 * 10**9
FIRST_COST = 18 * 10**9
AXES = ("space", "wt")
VMEM = pltpu.VMEM
SMEM = pltpu.SMEM
LANES = 128
F32 = jnp.float32
BF16 = jnp.bfloat16


def pieces(width):
    return [
        (p, p * LANES, min(LANES, width - p * LANES)) for p in range(-(-width // LANES))
    ]


def fill(wide, base, value):
    rows, width = value.shape
    for p, lane, lanes in pieces(width):
        wide[p, pl.ds(base, rows), 0:lanes] = value[:, lane : lane + lanes]


def surface_rows(side):
    return side**3 - (side - 2) ** 3


def folded_shape(side, lanes):
    rows, folds = surface_rows(side), LANES // lanes
    short = rows // folds // 16 * 16
    return folds, short, rows - folds * short


def folded_rows(side, width):
    rows = 0
    for p, lane, lanes in pieces(width):
        folds, short, left = folded_shape(side, lanes)
        rows += surface_rows(side) if folds == 1 else short + left
    return -(-rows // 16) * 16


def folded_start(side, width):
    rows = surface_rows(side) * (width // LANES)
    for p, lane, lanes in pieces(width):
        if lanes < LANES:
            rows += folded_shape(side, lanes)[2]
    return -(-rows // 16) * 16


def pack_surface(wide, out_ref, side, width, change=lambda value: value):
    plane = side * side
    last = side - 1
    rows = surface_rows(side)
    start = folded_start(side, width)
    whole = []
    for p, lane, lanes in pieces(width):
        ref = wide.at[p]
        parts = [ref[pl.ds(0, plane), :], ref[pl.ds(last * plane, plane), :]]
        for y in (0, last):
            for x in range(1, last):
                parts.append(ref[pl.ds(x * plane + y * side, side), :])
        for z in (0, last):
            for x in range(1, last):
                at = x * plane + side + z
                parts.append(ref[pl.ds(at, side - 2, stride=side), :])
        value = change(jnp.concatenate(parts, axis=0))
        folds, count, left = folded_shape(side, lanes)
        if folds == 1:
            whole.append(value)
            continue
        whole.append(value[folds * count :])
        result = value[:count]
        position = lax.broadcasted_iota(jnp.int32, (count, LANES), 1)
        for n in range(1, folds):
            part = pltpu.roll(value[n * count : (n + 1) * count], n * lanes, axis=1)
            result = jnp.where(position >= n * lanes, part, result)
        out_ref[pl.ds(start, count), :] = result.astype(BF16)
    value = jnp.concatenate(whole, axis=0)
    if value.shape[0] < start:
        rest = jnp.zeros((start - value.shape[0], LANES), F32)
        value = jnp.concatenate([value, rest], axis=0)
    out_ref[pl.ds(0, start), :] = value.astype(BF16)


def spread_surface(packed_ref, faces, slot, side, width):
    plane = side * side
    inner = (side - 2) * side
    last = side - 1
    base = slot * 6 * plane
    rows = surface_rows(side)
    start = folded_start(side, width)
    whole = packed_ref[pl.ds(0, start), :].astype(F32)
    for p, lane, lanes in pieces(width):
        ref = faces.at[p]
        folds, count, left = folded_shape(side, lanes)
        if folds == 1:
            part = whole[p * rows : (p + 1) * rows]
        else:
            part = packed_ref[pl.ds(start, count), :].astype(F32)
            turned = [part] + [
                pltpu.roll(part, LANES - n * lanes, axis=1) for n in range(1, folds)
            ]
            turned.append(whole[p * rows : p * rows + left])
            part = jnp.concatenate(turned, axis=0)
        ref[pl.ds(base, 2 * plane), :] = part[: 2 * plane]
        row = 2 * plane
        for f in (2, 3):
            ref[pl.ds(base + f * plane + side, inner), :] = part[row : row + inner]
            row += inner
        for f in (4, 5):
            for x in range(1, last):
                at = base + f * plane + x * side + 1
                ref[pl.ds(at, side - 2), :] = part[row : row + side - 2]
                row += side - 2
        for end, x in ((0, 0), (1, last)):
            for f, y in ((2, 0), (3, last)):
                ref[pl.ds(base + f * plane + x * side, side), :] = ref[
                    pl.ds(base + end * plane + y * side, side), :
                ]
            for f, z in ((4, 0), (5, last)):
                ref[pl.ds(base + f * plane + x * side, side), :] = ref[
                    pl.ds(base + end * plane + z, side, stride=side), :
                ]
        for f, z in ((4, 0), (5, last)):
            for g, y in ((2, 0), (3, last)):
                ref[pl.ds(base + f * plane + y, side, stride=side), :] = ref[
                    pl.ds(base + g * plane + z, side, stride=side), :
                ]


def cut_surface(wide, faces, slot, side):
    plane = side * side
    last = side - 1
    base = slot * 6 * plane
    for p in range(wide.shape[0]):
        for n, x in enumerate((0, last)):
            faces[p, pl.ds(base + n * plane, plane), :] = wide[
                p, pl.ds(x * plane, plane), :
            ]
        for n, y in ((2, 0), (3, last)):
            for x in range(side):
                faces[p, pl.ds(base + n * plane + x * side, side), :] = wide[
                    p, pl.ds(x * plane + y * side, side), :
                ]
        for n, z in ((4, 0), (5, last)):
            faces[p, pl.ds(base + n * plane, plane), :] = wide.at[p][
                pl.ds(z, plane, stride=side), :
            ]


def mark_kernel(out_ref):
    out_ref[...] = jnp.zeros(out_ref.shape, out_ref.dtype)


def pack_kernel(x_ref, mark, after, out_ref, *refs, side):
    *pieces_out, wide = refs
    fill(wide, 0, x_ref[...].astype(F32))
    pack_surface(wide, out_ref, side, x_ref.shape[1])
    share(x_ref[...], pieces_out)


def share(value, refs):
    for n, ref in enumerate(refs):
        count = ref.shape[0]
        ref[...] = value[n * count : (n + 1) * count]


def weight_rows(width, tap):
    return [
        (lane, 9 * lane + tap * lanes, lanes) for _, lane, lanes in pieces(width)
    ]


def weights_kernel(own_ref, other_ref, out_ref):
    core = lax.axis_index("wt")
    taps, depth, both = own_ref.shape
    width = out_ref.shape[2]
    half = depth * (both // width)
    step = 16
    for tap in range(taps):
        rows = {}
        for channel, row, count in weight_rows(width, tap % 9):
            for n in range(0, count, step):
                rows[channel + n] = row + n
        for ref, place in ((own_ref, core), (other_ref, 1 - core)):
            for group in range(both // width):
                lane = group * width
                value = ref[tap, :, lane : lane + width]
                for n in range(0, depth, step):
                    at = group * depth + n
                    row = jnp.where(place == 0, rows[at], rows[at + half])
                    row = pl.multiple_of(row, step)
                    out_ref[tap // 9, pl.ds(row, step), :] = value[n : n + step]


def tap_weights(w, tap):
    third, tap = divmod(tap, 9)
    return jnp.concatenate(
        [w[third, pl.ds(row, count), :] for _, row, count in weight_rows(w.shape[2], tap)],
        axis=0,
    )


def shifts(middle, low, high, mask):
    side = middle.shape[1]
    return (
        pltpu.roll(jnp.where(mask == side - 1, low, middle), 1, axis=1),
        middle,
        pltpu.roll(jnp.where(mask == 0, high, middle), side - 1, axis=1),
    )


def turned_chip(chips):
    chip = lax.axis_index("space")
    return ((chip == 0) | (chip == chips - 1)).astype(jnp.int32)


def inside_kernel(*refs, side, chips, counts, opening):
    refs = list(refs)
    table_refs, extra, *sources = [[refs.pop(0) for _ in range(n)] for n in counts]
    w, total, near, masks, ends, wide, faces, lhs, tables, semaphores = refs
    copies = [
        pltpu.make_async_copy(ref, tables.at[n], semaphores.at[n])
        for n, ref in enumerate(table_refs)
    ]
    for copy in copies:
        copy.start()
    width = w.shape[2]
    plane = side * side
    turned = turned_chip(chips)
    home = 2 * lax.axis_index("space") + lax.axis_index("wt")
    other = home + 1 - 2 * lax.axis_index("wt")
    away = jnp.where(turned == 1, other, home)
    ids = (home, other) if opening else (away, home + other - away)
    for slot, parts in enumerate(sources):
        for n, part in enumerate(parts):
            fill(wide.at[slot], n * part.shape[0], part[...].astype(F32))
    mask = lax.broadcasted_iota(jnp.int32, (side, side, LANES), 1)
    nothing = jnp.zeros((side, side, LANES), F32)
    edge = jnp.zeros((1, side, LANES), F32)
    for p, lane, lanes in pieces(width):
        folds = LANES // lanes
        for x in range(side):
            middle = wide[turned, p, pl.ds(x * plane, plane), :]
            middle = middle.reshape(side, side, LANES)
            if folds > 1:
                position = lax.broadcasted_iota(jnp.int32, middle.shape, 2)
                for n in range(1, folds):
                    moved = pltpu.roll(middle, n * lanes, axis=2)
                    middle = jnp.where(position >= n * lanes, moved, middle)
            moved = shifts(middle, nothing, nothing, mask)
            taps = []
            for j in range(3):
                for k in range(3):
                    value = moved[k]
                    if j == 0:
                        value = jnp.concatenate([edge, value[: side - 1]], axis=0)
                    elif j == 2:
                        value = jnp.concatenate([value[1:], edge], axis=0)
                    taps.append(value.reshape(plane, LANES))
            for t in range(0, 9, folds):
                value = taps[t]
                used = min(folds, 9 - t)
                for n in range(1, used):
                    position = lax.broadcasted_iota(jnp.int32, value.shape, 1)
                    value = jnp.where(position >= n * lanes, taps[t + n], value)
                at = 9 * lane + t * lanes
                lhs[pl.ds(x * plane, plane), at : at + used * lanes] = value[
                    :, : used * lanes
                ].astype(BF16)
    for i in (1, 0, 2):
        first, source, count = (1, 0, 0)[i], (0, 0, 1)[i], side - (i != 1)
        acc = jnp.dot(
            lhs[pl.ds(source * plane, count * plane), :],
            w[i],
            preferred_element_type=F32,
        )
        for p, lane, lanes in pieces(width):
            part = acc[:, lane : lane + lanes]
            place = pl.ds(first * plane, count * plane)
            if i == 1:
                for ref in extra:
                    part = part + ref[:, lane : lane + lanes].astype(F32)
                total[p, place, 0:lanes] = part
            else:
                total[p, place, 0:lanes] += part
    for p in range(total.shape[0]):
        for n, z in enumerate((0, side - 1)):
            ends[p, pl.ds(n * plane, plane), :] = total.at[p][
                pl.ds(z, plane, stride=side), :
            ]
    fill(faces, 0, jnp.zeros((6 * plane, width), F32))
    for slot in range(2):
        cut_surface(wide.at[slot], faces, slot + 1, side)
    for copy in copies:
        copy.wait()
    row = turned if opening else 0
    entries = [tables[row, 0, t] for t in range(27)]
    choose_near(entries, ids, faces, near, masks, side)


def borders(side):
    last = side - 1
    for group in range(6):
        axis, up = divmod(group, 2)
        face = 2 * axis + 1 - up
        sign = 2 * up - 1
        for to, count, row, b in (
            (0, 1, last * side, -1),
            (1, side, 0, 0),
            (side + 1, 1, 0, 1),
        ):
            offsets = {}
            for c in (-1, 0, 1):
                if axis == 0:
                    offsets[c] = (sign, b, c)
                elif axis == 1 and b == 0:
                    offsets[c] = (0, sign, c)
                elif axis == 2 and b == 0 and c == 0:
                    offsets[c] = (0, 0, sign)
            yield group, to, count, row, face, offsets


def entry(offset):
    a, b, c = offset
    return 9 * (a + 1) + 3 * (b + 1) + c + 1


def choose_near(entries, ids, faces, near, masks, side):
    plane = side * side

    def slot(n):
        here = jnp.where(n == ids[0], 1, jnp.where(n == ids[1], 2, 3))
        return jnp.where(n < 0, 0, here)

    slots = [slot(n) for n in entries]
    for t, value in enumerate(slots):
        flag = (value > 0 if t == 13 else value == 3).astype(F32)
        masks[pl.ds(8 * t, 8), :] = jnp.full((8, LANES), flag, F32)
    for group, to, count, row, face, offsets in borders(side):
        for c, offset in offsets.items():
            value = slots[entry(offset)]
            source = jnp.where(value == 3, 0, value)
            start = pl.multiple_of((source * 6 + face) * plane + row, side)
            place = pl.ds(((3 * group + c + 1) * (side + 2) + to) * side, count * side)
            for p in range(faces.shape[0]):
                near[p, place, :] = faces[p, pl.ds(start, count * side), :]


def add_outside(far, w, near, masks, ends, total, faces, even, odd, side):
    width = w.shape[2]
    plane = side * side
    last = side - 1
    spread_surface(far, faces, 0, side, width)
    mask = lax.broadcasted_iota(jnp.int32, (side, side, LANES), 1)
    for group, to, count, row, face, offsets in borders(side):
        for p, lane, lanes in pieces(width):
            place = pl.ds(to * side, count * side)
            if not offsets:
                blank = jnp.zeros((3, side, lanes), BF16)
                even[group, :, place, lane : lane + lanes] = blank
                continue

            def chunk(c):
                if c not in offsets:
                    return jnp.zeros((count, side, LANES), F32)
                away = masks[pl.ds(8 * entry(offsets[c]), 8), :] > 0
                at = ((3 * group + c + 1) * (side + 2) + to) * side
                afar = faces[p, pl.ds(face * plane + row, count * side), :]
                here = near[p, pl.ds(at, count * side), :]
                shape = (count, side, LANES)
                return jnp.where(
                    jnp.broadcast_to(away[None], shape),
                    afar.reshape(shape),
                    here.reshape(shape),
                )

            moved = shifts(chunk(0), chunk(-1), chunk(1), mask[:count])
            for k, value in enumerate(moved):
                value = value.reshape(count * side, LANES)[:, :lanes]
                if count == side:
                    odd[group, k, :, lane : lane + lanes] = value.astype(BF16)
                even[group, k, place, lane : lane + lanes] = value.astype(BF16)

    sums = [None] * 6
    for i in range(3):
        for j in range(3):
            for k in range(3):
                parts, groups = [], []
                for axis, tap, chunk, shift in ((0, i, j, k), (1, j, i, k), (2, k, i, j)):
                    if tap == 1:
                        continue
                    group = 2 * axis + tap // 2
                    if chunk == 1:
                        parts.append(odd[group, shift])
                    else:
                        parts.append(
                            even[group, shift, chunk * side : chunk * side + plane]
                        )
                    groups.append(group)
                if not parts:
                    continue
                product = jnp.dot(
                    jnp.concatenate(parts, axis=0),
                    tap_weights(w, 9 * i + 3 * j + k),
                    preferred_element_type=F32,
                )
                for n, group in enumerate(groups):
                    part = product[n * plane : (n + 1) * plane]
                    sums[group] = part if sums[group] is None else sums[group] + part

    for p, lane, lanes in pieces(width):
        ref = total.at[p]
        part = [value[:, lane : lane + lanes] for value in sums]
        if lanes < LANES:
            pad = jnp.zeros((plane, LANES - lanes), F32)
            part[4:] = [jnp.concatenate([value, pad], axis=1) for value in part[4:]]
        for up, z in ((0, 0), (1, last)):
            line = ends[p, pl.ds(up * plane, plane), :]
            ref[pl.ds(z, plane, stride=side), :] = line + part[4 + up]
        for up, x in ((0, 0), (1, last)):
            ref[pl.ds(x * plane, plane), 0:lanes] += part[up]
        for up, y in ((0, 0), (1, last)):
            for x in range(side):
                ref[pl.ds(x * plane + y * side, side), 0:lanes] += part[2 + up][
                    x * side : (x + 1) * side
                ]


def first_kernel(far, w, total_in, near, masks, ends, surface, *refs, side):
    *outs, total, faces, even, odd = refs
    add_outside(far, w, near, masks, ends, total, faces, even, odd, side)
    active = masks[pl.ds(8 * 13, 1), :]

    def change(value):
        return jnp.maximum(value, 0.0) * active[:, : value.shape[1]]

    pack_surface(total, surface, side, w.shape[2], change)
    for p, lane, lanes in pieces(w.shape[2]):
        for n, out in enumerate(outs):
            count = out.shape[0]
            value = change(total[p, pl.ds(n * count, count), 0:lanes])
            out[:, lane : lane + lanes] = value.astype(BF16)


def second_kernel(
    occupancy, far, w, total_in, near, masks, ends, out, total, faces, even, odd, *, side
):
    add_outside(far, w, near, masks, ends, total, faces, even, odd, side)
    active = occupancy[...].astype(F32)
    for p, lane, lanes in pieces(w.shape[2]):
        value = jnp.maximum(total[p, :, 0:lanes], 0.0)
        out[:, lane : lane + lanes] = value * active


def chip_exchanges(chips):
    def end(chip):
        return int(chip in (0, chips - 1))

    last = 2 * chips - 1
    first, second = [(0, 1), (last, last - 1)], [(1, 0), (last - 1, last)]
    for c in range(chips - 1):
        up, down = 2 * c, 2 * (c + 1)
        first.append((up + 1, down + end(c + 1)))
        first.append((down, up + 1 - end(c)))
        second.append((up + 1 - end(c), down))
        second.append((down + end(c + 1), up + 1))
    return first, second


def call(kernel, operands, outs, scratch=(), anywhere=0, cost=0, aliases={}):
    outs = [jax.ShapeDtypeStruct(shape, kind) for shape, kind in outs]
    result = pl.pallas_call(
        kernel,
        out_shape=outs,
        in_specs=[pl.BlockSpec(memory_space=pl.ANY)] * anywhere
        + [pl.BlockSpec(memory_space=VMEM)] * (len(operands) - anywhere),
        out_specs=[pl.BlockSpec(memory_space=VMEM)] * len(outs),
        scratch_shapes=list(scratch),
        input_output_aliases=aliases,
        compiler_params=pltpu.CompilerParams(vmem_limit_bytes=32 * 2**20),
        cost_estimate=pl.CostEstimate(flops=cost, bytes_accessed=0, transcendentals=0),
    )(*operands)
    return result[0] if len(outs) == 1 else result


def body(features, occupancy, neighbours, kernel_one, kernel_two):
    side, width = features.shape[1], features.shape[4]
    rows, plane = side**3, side * side
    total = lax.axis_size(AXES)
    halves = [(i, i ^ 1) for i in range(total)]
    chips = total // 2
    first, second = chip_exchanges(chips)
    face = ((folded_rows(side, width), LANES), BF16)
    piece = ((rows // PARTS, width), BF16)
    wide = ((rows, width), F32)
    count = len(pieces(width))

    own = features.reshape(rows, width)
    mark = call(mark_kernel, (), [((8, LANES), F32)], cost=MARK_COST)
    mark, one_late = lax.optimization_barrier((mark, kernel_one))
    after = call(mark_kernel, (), [((8, LANES), F32)], cost=NEXT_COST)
    own_face, *own_parts = call(
        functools.partial(pack_kernel, side=side),
        (own, mark, after),
        [face] + [piece] * PARTS,
        [VMEM((count, rows, LANES), F32)],
        cost=PACK_COST,
    )
    table_other = lax.ppermute(neighbours, AXES, halves)
    other = [lax.ppermute(part, AXES, halves) for part in own_parts]
    far = lax.ppermute(own_face, AXES, first)

    def weights(kernel, late):
        flat = kernel.reshape((27,) + kernel.shape[3:])
        swapped = lax.ppermute(late.reshape(flat.shape), AXES, halves)
        return call(weights_kernel, (flat, swapped), [((3, 9 * width, width), BF16)])

    w_one, w_two = weights(kernel_one, one_late), weights(kernel_two, kernel_two)

    sums = ((count, rows, LANES), F32)
    near = ((count, 6 * 3 * (side + 2) * side, LANES), F32)
    masks = ((27 * 8, LANES), F32)
    ends = ((count, 2 * plane, LANES), F32)

    def inside(layer, tables, extra, here, there, w):
        counts = (len(tables), len(extra), len(here), len(there))
        return call(
            functools.partial(
                inside_kernel, side=side, chips=chips, counts=counts, opening=layer == 0
            ),
            (*tables, *extra, *here, *there, w),
            [sums, near, masks, ends],
            [
                VMEM((2, count, rows, LANES), F32),
                VMEM((count, 3 * 6 * plane, LANES), F32),
                VMEM((rows, 9 * width), BF16),
                SMEM((len(tables),) + neighbours.shape, jnp.int32),
                pltpu.SemaphoreType.DMA((len(tables),)),
            ],
            anywhere=len(tables),
        )

    planes = [
        VMEM((count, 6 * plane, LANES), F32),
        VMEM((6, 3, plane + 2 * side, width), BF16),
        VMEM((6, 3, plane, width), BF16),
    ]
    hidden_face, *hidden, _ = call(
        functools.partial(first_kernel, side=side),
        (far, w_one, *inside(0, (neighbours, table_other), (), own_parts, other, w_one)),
        [face] + [piece] * PARTS + [sums],
        planes,
        aliases={2: 1 + PARTS},
        cost=FIRST_COST,
    )
    hidden_other = [lax.ppermute(part, AXES, halves) for part in hidden]
    hidden_far = lax.ppermute(hidden_face, AXES, second)
    out, _ = call(
        functools.partial(second_kernel, side=side),
        (
            occupancy.reshape(1, 1),
            hidden_far,
            w_two,
            *inside(1, (neighbours,), (own,), hidden, hidden_other, w_two),
        ),
        [wide, sums],
        planes,
        aliases={3: 1},
    )
    return out.reshape((1, side, side, side, width))


def solution(mesh):
    return jax.shard_map(
        body,
        mesh=mesh,
        in_specs=(
            P(AXES, None, None, None, None),
            P(AXES),
            P(AXES, None),
            P(None, None, None, None, "wt"),
            P(None, None, None, None, "wt"),
        ),
        out_specs=P(AXES, None, None, None, None),
        check_vma=False,
    )
```
